32 devices in a mesh: grp: 4 (over z), seq: 8 (over y, x, core).
Axes of the slice: x: 2, y: 2, z: 4, core: 2. Of those that a mesh axis runs over, the one named last changes fastest.
Arguments:
- queries: bfloat16 [32, 4, 64, 576], P('grp'), parts along dimension 0, may hold values from -190 to 190
- latent_cache: bfloat16 [32, 8192, 576], P('grp', 'seq'), parts along dimension 0, may hold values from -4 to 4
- context_lengths: int32 [32], P('grp'), parts along dimension 0, may hold values from 2048 to 8192, as said below
- value_up: bfloat16 [64, 512, 128], P('seq'), may hold values from -0.5 to 0.5
- output_projection_rows: bfloat16 [8192, 7168], P('seq'), may hold values from -0.25 to 0.25
Outputs:
- attention_out: bfloat16 [32, 4, 7168], P('grp', None, 'seq'), parts along dimension 0
The draws below stay inside these ranges and needn't reach their ends.
There are 4 independent parts, one for each index of `grp`. The reference program is written for one: setup_inputs(seed, part) draws one part's arguments, and reference() takes and returns one part's arrays. A program takes and returns all parts, laid end to end along the dimension named above; an argument that names none is the same for every part. Nothing has to cross between parts.
Inputs may be any that keep to these rules, and one draw needn't show every extreme that they name: `context_lengths`: in every draw one request holds exactly 8192 tokens.
All inputs are finite; a program needn't handle non-finite values.
Results may differ from the reference program's by a relative error of at most 0.0058.
Values sent between devices are 32-bit elements; how exact they have to be, the bound alone decides.
No kernel may reach another device: no remote copies, remote signals or barrier semaphores. Data moves between devices by JAX's collectives and lax.ppermute only.
A program may use at most 128 MiB of HBM per device.

```python
import jax
import jax.numpy as jnp
from jax import lax

B = 8
NQ = 4
CTX_DEV = 1024
H = 64
KVR = 512
VD = 128
D = 7168
LAT = 576
CTX = 8192
N_SEQ = 8


def draw_queries(key, part):
    own_key = jax.random.fold_in(key, 7)
    queries = 1.5 * jnp.clip(jax.random.normal(own_key, (B, NQ, H, LAT), jnp.float32), -4.0, 4.0)
    return queries.astype(jnp.bfloat16)


def draw_latent_cache(key, part):
    own_key = jax.random.fold_in(key, 5)
    latent = jnp.clip(jax.random.normal(own_key, (B, CTX, LAT), jnp.float32), -4.0, 4.0)
    return latent.astype(jnp.bfloat16)


def draw_context_lengths(key, part):
    own_key = jax.random.fold_in(key, 3)
    key_draw, key_order = jax.random.split(own_key, 2)
    lengths = jax.random.randint(key_draw, (B,), CTX // 4, CTX + 1)
    longest = jax.random.randint(key_order, (), 0, B)
    lengths = lengths.at[longest].set(CTX)
    return lengths.astype(jnp.int32)


def level_of(key, shape, shards, smallest, high):
    factor_of, own = 1.0, jax.random.fold_in(key, 6)
    for axis_at, shards_of in shards:
        heights = jnp.exp(jax.random.uniform(jax.random.fold_in(own, axis_at), (shards_of,), jnp.float32, smallest / len(shards), high / len(shards)))
        factor_of = factor_of * jnp.repeat(heights, shape[axis_at] // shards_of).reshape([-1 if axis == axis_at else 1 for axis in range(len(shape))])
    return factor_of


def gaussian(rng, shape, scale, limit, shards=(), held_as=jnp.bfloat16):
    array = scale * jax.random.normal(rng, shape, jnp.float32)
    if shards:
        array = array * level_of(rng, shape, shards, -0.22, 0.18)
    return jnp.clip(array, -limit, limit).astype(held_as)


def setup_inputs(seed: int = 0, part: int = 0) -> dict:
    streams_of = jax.random.split(jax.random.key(seed), 6)
    own_keys = jax.random.split(jax.random.fold_in(streams_of[5], part), 6)
    queries = draw_queries(jax.random.fold_in(jax.random.fold_in(streams_of[5], part), 71), part)
    latent_cache = draw_latent_cache(jax.random.fold_in(jax.random.fold_in(streams_of[5], part), 71), part)
    context_lengths = draw_context_lengths(jax.random.fold_in(jax.random.fold_in(streams_of[5], part), 71), part)
    value_up = gaussian(streams_of[3], (H, KVR, VD), (KVR // 4) ** -0.5, 0.5, ((0, 8),))
    output_projection_rows = gaussian(streams_of[4], (H * VD, D), (H * VD // 16) ** -0.5, 0.25, ((0, 8),))
    return dict(queries=queries, latent_cache=latent_cache, context_lengths=context_lengths, value_up=value_up, output_projection_rows=output_projection_rows)


score_scale = 0.07216878364870323
empty_mark = -1.0e30


def local_partial(queries, cache_rows, context_lengths, first_token):
    query_count = queries.shape[1]
    shard_width = cache_rows.shape[1]
    scores = jnp.einsum("bqhc,btc->bqht", queries.astype(jnp.float32), cache_rows.astype(jnp.float32)) * score_scale
    position = first_token + jnp.arange(shard_width, dtype=jnp.int32)
    row_limit = context_lengths[:, None] - (query_count - 1) + jnp.arange(query_count, dtype=jnp.int32)[None, :]
    visible = position[None, None, None, :] < row_limit[:, :, None, None]
    masked = jnp.where(visible, scores, empty_mark)
    row_peak = jnp.max(masked, axis=3)
    weights = jnp.where(visible, jnp.exp(masked - row_peak[..., None]), 0.0)
    row_rescale = jnp.maximum(jnp.sum(weights, axis=3), 1.0)
    weights_low = lax.optimization_barrier(weights.astype(jnp.bfloat16)).astype(jnp.float32)
    values = jnp.einsum("bqht,btc->bqhc", weights_low, cache_rows[:, :, :KVR].astype(jnp.float32))
    return values / row_rescale[..., None], row_peak + jnp.log(row_rescale)


def reference(queries, latent_cache, context_lengths, value_up, output_projection_rows):
    def device_partial_terms(shard_index):
        first_token = shard_index * CTX_DEV
        cache_rows = lax.dynamic_slice_in_dim(latent_cache, first_token, CTX_DEV, 1)
        return local_partial(queries, cache_rows, context_lengths, first_token)

    partials, log_sums = lax.map(device_partial_terms, jnp.arange(N_SEQ, dtype=jnp.int32))
    greatest_score = jnp.max(log_sums, axis=0)
    shares = jnp.exp(log_sums - greatest_score[None])
    attended = jnp.sum(shares[..., None] * partials, axis=0) / jnp.sum(shares, axis=0)[..., None]
    attended_low = lax.optimization_barrier(attended.astype(jnp.bfloat16)).astype(jnp.float32)
    head_out = jnp.einsum("bqhc,hcv->bqhv", attended_low, value_up.astype(jnp.float32))
    head_low = lax.optimization_barrier(head_out.astype(jnp.bfloat16)).astype(jnp.float32)
    flattened_heads = head_low.reshape(head_low.shape[0], head_low.shape[1], -1)
    final_output = jnp.einsum("msp,pc->msc", flattened_heads, output_projection_rows.astype(jnp.float32))
    return final_output.astype(jnp.bfloat16)
```

```python
import functools
import math

import jax
import jax.numpy as jnp
from jax import lax
from jax.experimental import pallas as pl
from jax.experimental.pallas import tpu as pltpu
from jax.sharding import PartitionSpec as P

score_scale = 0.07216878364870323
empty_mark = -1e30
MIB = 1024 * 1024
PARTS = (2, 2, 2, 2)
LAST = (50, 50, 0)
DIRECT = ()
ORDER = "A0:10 A1:10 C0:50 A2:10 C1:50 A3:10 C2:50 S0:50 C3:0 S1:0 S2:0 S3:50 M0:5 M1:5 M2:5"
BLOCK = 32
PIECES = 4
TILE = 256
OWN = 8
VM = pl.BlockSpec(memory_space=pltpu.VMEM)
SM = pl.BlockSpec(memory_space=pltpu.SMEM)
HB = pl.BlockSpec(memory_space=pltpu.HBM)
ANY = pl.BlockSpec(memory_space=pl.ANY)


def declared(length):
    return pl.CostEstimate(flops=length * 10**8 + 1, bytes_accessed=1, transcendentals=0)


def group(me, q, mate, turn):
    core = (me & 1) ^ mate ^ turn
    first = 2 + 2 * core
    return me ^ mate ^ ((q >> 1) * first + (q & 1) * (6 - first))


def pairs_of(n, step, turn):
    bits = ((1, 1), (2, 4), (4, 2), (6, 6))[step]
    return [(s, s ^ bits[(s & 1) ^ turn]) for s in range(n)]


def attention_kernel(first, count, turn, ready, following, after, me_ref, lengths_hbm, q_hbm, cache_hbm, *refs):
    q_buf, cache_buf = refs[:2] if ready else refs[-3:-1]
    refs = refs[2 * ready + after :]
    (keep, send), refs = refs[:2], refs[2:]
    targets, refs = refs[: 2 * (following > 0)], refs[2 * (following > 0) :]
    raw_buf, low_buf, acc_buf, lengths, length_sem, next_sems = refs[:6]
    nq, heads, lat = q_hbm.shape[1:]
    rows = nq * heads
    tokens = cache_hbm.shape[2]
    kvr = keep.shape[1]
    me = me_ref[0]
    length_copy = pltpu.make_async_copy(lengths_hbm, lengths, length_sem)
    length_copy.start()
    depth = lat // PIECES

    def copies(i, q_target, cache_target, sems):
        pieces = [slice(k * depth, (k + 1) * depth) for k in range(PIECES)]
        return [
            pltpu.make_async_copy(cache_hbm.at[first + i, piece], cache_target.at[piece], sems.at[k])
            for k, piece in enumerate(pieces)
        ] + [pltpu.make_async_copy(q_hbm.at[first + i], q_target, sems.at[PIECES])]

    ahead = [
        copy
        for i in range(following)
        for copy in copies(count + i, targets[0].at[i], targets[1].at[i], next_sems.at[i])
    ]
    fetches = []
    if not ready:
        fetches = [copies(i, q_buf.at[i], cache_buf.at[i], refs[-1].at[i]) for i in range(count)]
    for copy in sum(fetches, []) or ahead:
        copy.start()
    row = lax.broadcasted_iota(jnp.int32, (BLOCK, 1), 0)
    token = lax.broadcasted_iota(jnp.int32, (BLOCK, tokens), 1)
    lane = lax.broadcasted_iota(jnp.int32, (BLOCK, 128), 1)
    for out in (keep, send):
        out[out.shape[0] - OWN :, :] = jnp.zeros((OWN, kvr), jnp.float32)
    length_copy.wait()

    def score_piece(i, start):
        if fetches and start == 0:
            for copy in fetches[i]:
                copy.wait()
            for copy in ahead if i == 0 else ():
                copy.start()
        columns = slice(start, start + TILE)
        raw_buf[i % 2, :, columns] = jnp.dot(
            q_buf[i].reshape(rows, lat),
            cache_buf[i, :, columns],
            preferred_element_type=jnp.float32,
        )

    scales = {}
    tails = {}

    def weight_piece(i, start):
        block = slice(start, start + BLOCK)
        limit = lengths[first + i] - (nq - 1) - me * tokens + (row + start) // heads
        raw = jnp.where(token < limit, raw_buf[i % 2, block, :], empty_mark)
        peak = jnp.max(raw, axis=1, keepdims=True)
        weights = jnp.exp2((raw - peak) * (score_scale * math.log2(math.e)))
        total = jnp.maximum(jnp.sum(weights, axis=1, keepdims=True), 1.0)
        low_buf[i % 2, block, :] = weights.astype(jnp.bfloat16)
        some = limit > 0
        scales[i, start] = jnp.where(some, 1.0 / total, 0.0)
        lse = jnp.where(some, peak * score_scale + jnp.log(total), empty_mark)
        part = start // 128
        spread = jnp.where(lane + part * 128 == row + start, lse, 0.0)
        tails[i, part] = tails.get((i, part), 0.0) + jnp.sum(spread, axis=0, keepdims=True)

    def value_piece(i, start):
        acc = lax.dot_general(
            low_buf[i % 2],
            cache_buf[i, start : start + TILE, :],
            (((1,), (1,)), ((), ())),
            preferred_element_type=jnp.float32,
        )
        for block in range(0, rows, BLOCK):
            acc_buf[i % 2, block : block + BLOCK, start : start + TILE] = acc[block : block + BLOCK] * scales[i, block]

    def out_piece(i):
        for mate, out in enumerate((keep, send)):
            for q in range(4):
                for j in range(nq):
                    source = pl.multiple_of(j * heads + group(me, q, mate, turn) * OWN, OWN)
                    to = ((q * count + i) * nq + j) * OWN
                    out[to : to + OWN, :] = acc_buf[i % 2, pl.ds(source, OWN), :]
        for part in range(rows // 128):
            for out in (keep, send):
                at = out.shape[0] - OWN + i
                out[at : at + 1, part * 128 : (part + 1) * 128] = tails[i, part]

    def pieces(stage, i):
        if not 0 <= i < count:
            return []
        if stage == 0:
            return [functools.partial(score_piece, i, t) for t in range(0, tokens, TILE)]
        if stage == 1:
            return [functools.partial(weight_piece, i, t) for t in range(0, rows, BLOCK)]
        return [functools.partial(value_piece, i, t) for t in range(0, kvr, TILE)] + [functools.partial(out_piece, i)]

    for i in range(count + 2):
        stages = [pieces(stage, i - stage) for stage in range(3)]
        marked = []
        for stage, own in enumerate(stages):
            marked += [((k + 0.5) / len(own), stage, k, piece) for k, piece in enumerate(own)]
        for _, _, _, piece in sorted(marked, key=lambda entry: entry[:3]):
            piece()
    for copy in ahead:
        copy.wait()


def attention(me, lengths, queries, cache, kvr, first, count, turn, ready, following, after, length):
    batch, nq, heads, lat = queries.shape
    tokens = cache.shape[2]
    rows = nq * heads
    out_rows = count * rows // 2 + OWN
    scratch = [
        pltpu.VMEM((2, rows, tokens), jnp.float32),
        pltpu.VMEM((2, rows, tokens), jnp.bfloat16),
        pltpu.VMEM((2, rows, kvr), jnp.float32),
        pltpu.SMEM((batch,), jnp.int32),
        pltpu.SemaphoreType.DMA,
        pltpu.SemaphoreType.DMA((max(following, 1), PIECES + 1)),
    ]
    if not ready:
        scratch += [
            pltpu.VMEM((count, nq, heads, lat), jnp.bfloat16),
            pltpu.VMEM((count, lat, tokens), jnp.bfloat16),
            pltpu.SemaphoreType.DMA((count, PIECES + 1)),
        ]
    out_shape = [jax.ShapeDtypeStruct((out_rows, kvr), jnp.float32)] * 2
    if following:
        out_shape += [
            jax.ShapeDtypeStruct((following, nq, heads, lat), jnp.bfloat16),
            jax.ShapeDtypeStruct((following, lat, tokens), jnp.bfloat16),
        ]
    return pl.pallas_call(
        functools.partial(attention_kernel, first, count, turn, len(ready) > 0, following, len(after)),
        in_specs=[SM, HB, HB, HB] + [VM] * len(ready) + [ANY] * len(after),
        out_specs=[VM] * len(out_shape),
        out_shape=out_shape,
        scratch_shapes=scratch,
        compiler_params=pltpu.CompilerParams(vmem_limit_bytes=24 * MIB),
        cost_estimate=declared(length),
    )(me, lengths, queries, cache, *ready, *after)


def merged(refs, shares):
    lanes = shares.shape[1]
    logs = [ref[ref.shape[0] - OWN :, :lanes] for ref in refs]
    largest = functools.reduce(jnp.maximum, logs)
    parts = [jnp.exp(log - largest) for log in logs]
    total = sum(parts[1:], parts[0])
    for k, part in enumerate(parts):
        shares[k] = (part / total).T
    return largest + jnp.log(total)


def merged_rows(refs, shares, me, heads, batch, q, b, j, turn):
    at = pl.ds(pl.multiple_of(j * heads + group(me, q, 0, turn) * OWN, OWN), OWN)
    source = ((q * batch + b) * (shares.shape[1] // heads) + j) * OWN
    rows = slice(source, source + OWN)
    terms_of = [shares[k, at, b : b + 1] * ref[rows, :] for k, ref in enumerate(refs)]
    return sum(terms_of[1:], terms_of[0])


def combine_kernel(places, pieces, batch, heads, turn, me_ref, keep_ref, got_ref, *refs):
    *outs, shares = refs[len(refs) - pieces - 1 :]
    lse = merged((keep_ref, got_ref), shares)
    lanes = shares.shape[1]
    size = batch * (lanes // heads) * OWN
    for q in range(places):
        side, at = divmod(q, places // pieces)
        for b in range(batch):
            for j in range(lanes // heads):
                to = at * size + (b * (lanes // heads) + j) * OWN
                outs[side][to : to + OWN, :] = merged_rows(
                    (keep_ref, got_ref), shares, me_ref[0], heads, batch, q, b, j, turn
                )
    for out in outs:
        out[out.shape[0] - OWN :, :] = jnp.zeros((OWN, out.shape[1]), jnp.float32)
        out[out.shape[0] - OWN :, :lanes] = lse


def combine(me, keep, got, places, pieces, batch, heads, lanes, turn, after, length):
    out_rows = (keep.shape[0] - OWN) // pieces + OWN
    return pl.pallas_call(
        functools.partial(combine_kernel, places, pieces, batch, heads, turn),
        in_specs=[SM, VM, VM] + [ANY] * len(after),
        out_specs=[VM] * pieces,
        out_shape=[jax.ShapeDtypeStruct((out_rows, keep.shape[1]), jnp.float32)] * pieces,
        scratch_shapes=[pltpu.VMEM((2, lanes, OWN), jnp.float32)],
        compiler_params=pltpu.CompilerParams(vmem_limit_bytes=16 * MIB),
        cost_estimate=declared(length),
    )(me, keep, got, *after)


def order_kernel(*refs):
    refs[-1][...] = jnp.zeros(refs[-1].shape, jnp.float32)


def order(after, length):
    return pl.pallas_call(
        order_kernel,
        in_specs=[ANY] * len(after),
        out_specs=VM,
        out_shape=jax.ShapeDtypeStruct((OWN, 128), jnp.float32),
        compiler_params=pltpu.CompilerParams(vmem_limit_bytes=MIB),
        cost_estimate=declared(length),
    )(*after)


def attend_rows(batch, heads, me, refs, shares, attended):
    merged(refs, shares)
    positions = shares.shape[1] // heads
    for b in range(batch):
        for j in range(positions):
            to = (b * positions + j) * OWN
            rows = merged_rows(refs, shares, me, heads, batch, 0, b, j, 0)
            for k in range(attended.shape[0]):
                attended[k, to : to + OWN, :] = rows[:, k * 128 : (k + 1) * 128]


def last_merge_kernel(batch, heads, count, me_ref, *refs):
    out_ref, shares = refs[-2:]
    attend_rows(batch, heads, me_ref[0], refs[:count], shares, out_ref)


def last_merge(me, arrays, batch, heads, lanes, after, length):
    rows, kvr = arrays[0].shape
    return pl.pallas_call(
        functools.partial(last_merge_kernel, batch, heads, len(arrays)),
        in_specs=[SM] + [VM] * len(arrays) + [ANY] * len(after),
        out_specs=VM,
        out_shape=jax.ShapeDtypeStruct((kvr // 128, rows - OWN, 128), jnp.float32),
        scratch_shapes=[pltpu.VMEM((len(arrays), lanes, OWN), jnp.float32)],
        compiler_params=pltpu.CompilerParams(vmem_limit_bytes=16 * MIB),
        cost_estimate=declared(length),
    )(me, *arrays, *after)


def heads_kernel(batch, heads, count, me_ref, *refs):
    early, refs = refs[: -count - 4], refs[-count - 4 :]
    arrays, (up_ref, out_ref, shares, attended) = refs[:count], refs[count:]
    attend_rows(batch, heads, me_ref[0], arrays, shares, attended)
    width = up_ref.shape[2]
    for i in range(OWN):
        own = [
            jnp.concatenate([ref[k, pl.ds(i, ref.shape[1] // OWN, stride=OWN), :] for k in range(ref.shape[0])], axis=1)
            for ref in (*early, attended)
        ]
        own = jnp.concatenate(own, axis=0).astype(jnp.bfloat16)
        head_out = jnp.dot(own, up_ref[i], preferred_element_type=jnp.float32)
        out_ref[:, i * width : (i + 1) * width] = head_out.astype(jnp.bfloat16)


def heads_out(me, early, arrays, batch, value_up, heads, lanes):
    rows, kvr = arrays[0].shape
    shape = (kvr // 128, rows - OWN, 128)
    places = sum(array.shape[1] for array in early) // OWN + shape[1] // OWN
    return pl.pallas_call(
        functools.partial(heads_kernel, batch, heads, len(arrays)),
        in_specs=[SM] + [VM] * (len(early) + len(arrays) + 1),
        out_specs=VM,
        out_shape=jax.ShapeDtypeStruct((places, OWN * value_up.shape[2]), jnp.bfloat16),
        scratch_shapes=[pltpu.VMEM((len(arrays), lanes, OWN), jnp.float32), pltpu.VMEM(shape, jnp.float32)],
        compiler_params=pltpu.CompilerParams(vmem_limit_bytes=16 * MIB),
        cost_estimate=declared(0),
    )(me, *early, *arrays, value_up)


def terms_kernel(mate, places, me_ref, heads_ref, weights_ref, *refs):
    out_ref = refs[-1]
    heads = heads_ref[...]
    width = out_ref.shape[2]
    for at, q in enumerate(places):
        start = pl.multiple_of(group(me_ref[0], q, mate, 0) * width, width)
        out_ref[at] = jnp.dot(heads, weights_ref[:, pl.ds(start, width)], preferred_element_type=jnp.float32)


def terms(me, heads, weights, mate, places, width, after, length):
    return pl.pallas_call(
        functools.partial(terms_kernel, mate, places),
        in_specs=[SM, VM, VM] + [ANY] * len(after),
        out_specs=VM,
        out_shape=jax.ShapeDtypeStruct((len(places), heads.shape[0], width), jnp.float32),
        compiler_params=pltpu.CompilerParams(vmem_limit_bytes=20 * MIB),
        cost_estimate=declared(length),
    )(me, heads, weights, *after)


def fold_kernel(own_ref, got_ref, *refs):
    for q, out in enumerate(refs[len(refs) - own_ref.shape[0] :]):
        out[...] = own_ref[q] + got_ref[q]


def fold(own, got, after):
    return pl.pallas_call(
        fold_kernel,
        in_specs=[VM, VM] + [ANY] * len(after),
        out_specs=[VM] * own.shape[0],
        out_shape=[jax.ShapeDtypeStruct(own.shape[1:], jnp.float32)] * own.shape[0],
        compiler_params=pltpu.CompilerParams(vmem_limit_bytes=8 * MIB),
        cost_estimate=declared(0),
    )(own, got, *after)


def finish_kernel(*refs):
    ins, out_ref = refs[:-1], refs[-1]
    batch, nq, _ = out_ref.shape
    total = ins[0][...]
    for ref in ins[1:]:
        total = total + ref[...]
    total = total.astype(jnp.bfloat16)
    for b in range(batch):
        out_ref[b] = total[b * nq : (b + 1) * nq, :]


def finish(terms_of, batch, nq):
    return pl.pallas_call(
        finish_kernel,
        in_specs=[VM] * len(terms_of),
        out_specs=VM,
        out_shape=jax.ShapeDtypeStruct((batch, nq, terms_of[0].shape[1]), jnp.bfloat16),
        compiler_params=pltpu.CompilerParams(vmem_limit_bytes=8 * MIB),
        cost_estimate=declared(0),
    )(*terms_of)


def local(n, queries, latent_cache, context_lengths, value_up, output_projection_rows):
    batch, nq, heads, _ = queries.shape
    kvr = value_up.shape[1]
    lanes = nq * heads
    me = lax.axis_index("seq").astype(jnp.int32).reshape(1)
    queries = pltpu.with_memory_space_constraint(queries, pltpu.HBM)
    cache = pltpu.with_memory_space_constraint(jnp.swapaxes(latent_cache, 1, 2), pltpu.HBM)
    lengths = pltpu.with_memory_space_constraint(context_lengths, pltpu.HBM)

    def swap(array, step, turn=0):
        return lax.ppermute(array, "seq", pairs_of(n, step, turn))

    keep, send, early = {}, {}, {}

    def arrived(p):
        turn = p & 1
        if len(send[p]) == 1:
            return [keep[p], swap(send[p][0], 2, turn)]
        second, first, both = send[p]
        return [keep[p], swap(first, 1, turn), swap(second, 2, turn), swap(both, 3, turn)]

    after, ready = (), ()
    for entry in ORDER.split():
        kind, p, length = entry[0], int(entry[1]), int(entry[3:])
        turn = p & 1
        if kind == "N":
            after = (order(after, length),)
        elif kind == "A":
            following = (*PARTS, 0)[p + 1]
            outs = attention(
                me, lengths, queries, cache, kvr, sum(PARTS[:p]), PARTS[p], turn, ready, following, after, length
            )
            keep[p], send[p], ready = outs[0], outs[1:2], outs[2:]
            after = (keep[p],)
        elif kind == "M":
            early[p] = last_merge(me, arrived(p), PARTS[p], heads, lanes, after, length)
            after = (early[p],)
        else:
            step = "CS".index(kind)
            pieces = 4 if kind == "C" and p in DIRECT else 2
            keep[p], *send[p] = combine(
                me,
                keep[p],
                swap(send[p][0], step, turn),
                4 >> step,
                pieces,
                PARTS[p],
                heads,
                lanes,
                turn,
                after,
                length,
            )
            after = (keep[p],)

    last = len(PARTS) - 1
    flat = heads_out(me, [early[p] for p in range(last)], arrived(last), PARTS[last], value_up, heads, lanes)
    width = output_projection_rows.shape[1] // n
    sums = {}
    after = ()
    for places in ((3, 2), (1, 0)):
        sent = terms(me, flat, output_projection_rows, 1, places, width, after, LAST[0])
        own = terms(me, flat, output_projection_rows, 0, places, width, (sent,), LAST[1])
        after = (order((own,), LAST[2]),) if LAST[2] and after else ()
        folded = fold(own, swap(sent, 0), after)
        sums.update(zip(places, folded))
        after = (folded[0],)
    return finish([sums[0], swap(sums[3], 3), swap(sums[2], 1), swap(sums[1], 2)], batch, nq)


def plain(queries, latent_cache, context_lengths, value_up, output_projection_rows):
    batch, nq = queries.shape[:2]
    kvr = value_up.shape[1]
    tokens = latent_cache.shape[1]
    scores = score_scale * jnp.einsum("bqhc,btc->bqht", queries, latent_cache, preferred_element_type=jnp.float32)
    position = lax.axis_index("seq") * tokens + jnp.arange(tokens, dtype=jnp.int32)
    limit = context_lengths[:, None] - (nq - 1) + jnp.arange(nq, dtype=jnp.int32)[None, :]
    visible = position[None, None, None, :] < limit[:, :, None, None]
    masked = jnp.where(visible, scores, empty_mark)
    peak = jnp.max(masked, axis=3)
    weights = jnp.where(visible, jnp.exp(masked - peak[..., None]), 0.0)
    total = jnp.maximum(jnp.sum(weights, axis=3), 1.0)
    values = jnp.einsum(
        "bqht,btc->bqhc", weights.astype(jnp.bfloat16), latent_cache[:, :, :kvr], preferred_element_type=jnp.float32
    )
    partials = lax.all_to_all((values / total[..., None])[None], "seq", split_axis=3, concat_axis=0, tiled=True)
    lse = lax.all_to_all((peak + jnp.log(total))[None], "seq", split_axis=3, concat_axis=0, tiled=True)
    shares = jnp.exp(lse - jnp.max(lse, axis=0)[None])
    attended = jnp.sum(shares[..., None] * partials, axis=0) / jnp.sum(shares, axis=0)[..., None]
    head_out = jnp.einsum(
        "bqhc,hcv->bqhv", attended.astype(jnp.bfloat16), value_up, preferred_element_type=jnp.float32
    )
    flat = head_out.astype(jnp.bfloat16).reshape(batch, nq, -1)
    term = jnp.einsum("msp,pc->msc", flat, output_projection_rows, preferred_element_type=jnp.float32)
    return lax.psum_scatter(term, "seq", scatter_dimension=2, tiled=True).astype(jnp.bfloat16)


def solution(mesh):
    n = mesh.shape["seq"]

    def body(queries, latent_cache, context_lengths, value_up, output_projection_rows):
        args = (queries, latent_cache, context_lengths, value_up, output_projection_rows)
        if n == 8 and value_up.shape[0] == OWN:
            return local(n, *args)
        return plain(*args)

    placed = (
        P("grp", None, None, None),
        P("grp", "seq", None),
        P("grp"),
        P("seq", None, None),
        P("seq", None),
    )
    return jax.shard_map(
        body, mesh=mesh, in_specs=placed, out_specs=P("grp", None, "seq"), check_vma=False
    )
```

```python
import functools
import math

import jax
import jax.numpy as jnp
from jax import lax
from jax.experimental import pallas as pl
from jax.experimental.pallas import tpu as pltpu
from jax.sharding import PartitionSpec as P

score_scale = 0.07216878364870323
empty_mark = -1e30
MIB = 1024 * 1024
PARTS = (2, 2, 2, 2)
LAST = (20, 20, 0)
DIRECT = ()
ORDER = "A0:10 A1:10 C0:50 A2:10 C1:50 A3:10 C2:50 S0:50 C3:0 S1:0 S2:0 S3:50 M0:5 M1:5 M2:5"
BLOCK = 32
PIECES = 4
TILE = 256
OWN = 8
VM = pl.BlockSpec(memory_space=pltpu.VMEM)
SM = pl.BlockSpec(memory_space=pltpu.SMEM)
HB = pl.BlockSpec(memory_space=pltpu.HBM)
ANY = pl.BlockSpec(memory_space=pl.ANY)


def declared(length):
    return pl.CostEstimate(flops=length * 10**8 + 1, bytes_accessed=1, transcendentals=0)


def group(me, q, mate, turn):
    core = (me & 1) ^ mate ^ turn
    first = 2 + 2 * core
    return me ^ mate ^ ((q >> 1) * first + (q & 1) * (6 - first))


def pairs_of(n, step, turn):
    bits = ((1, 1), (2, 4), (4, 2), (6, 6))[step]
    return [(s, s ^ bits[(s & 1) ^ turn]) for s in range(n)]


def attention_kernel(first, count, turn, ready, following, after, me_ref, lengths_hbm, q_hbm, cache_hbm, *refs):
    q_buf, cache_buf = refs[:2] if ready else refs[-3:-1]
    refs = refs[2 * ready + after :]
    (keep, send), refs = refs[:2], refs[2:]
    targets, refs = refs[: 2 * (following > 0)], refs[2 * (following > 0) :]
    raw_buf, low_buf, acc_buf, lengths, length_sem, next_sems = refs[:6]
    nq, heads, lat = q_hbm.shape[1:]
    rows = nq * heads
    tokens = cache_hbm.shape[2]
    kvr = keep.shape[1]
    me = me_ref[0]
    length_copy = pltpu.make_async_copy(lengths_hbm, lengths, length_sem)
    length_copy.start()
    depth = lat // PIECES

    def copies(i, q_target, cache_target, sems):
        pieces = [slice(k * depth, (k + 1) * depth) for k in range(PIECES)]
        return [
            pltpu.make_async_copy(cache_hbm.at[first + i, piece], cache_target.at[piece], sems.at[k])
            for k, piece in enumerate(pieces)
        ] + [pltpu.make_async_copy(q_hbm.at[first + i], q_target, sems.at[PIECES])]

    ahead = [
        copy
        for i in range(following)
        for copy in copies(count + i, targets[0].at[i], targets[1].at[i], next_sems.at[i])
    ]
    fetches = []
    if not ready:
        fetches = [copies(i, q_buf.at[i], cache_buf.at[i], refs[-1].at[i]) for i in range(count)]
    for copy in sum(fetches, []) or ahead:
        copy.start()
    row = lax.broadcasted_iota(jnp.int32, (BLOCK, 1), 0)
    token = lax.broadcasted_iota(jnp.int32, (BLOCK, tokens), 1)
    lane = lax.broadcasted_iota(jnp.int32, (BLOCK, 128), 1)
    for out in (keep, send):
        out[out.shape[0] - OWN :, :] = jnp.zeros((OWN, kvr), jnp.float32)
    length_copy.wait()

    def score_piece(i, start):
        if fetches and start == 0:
            for copy in fetches[i]:
                copy.wait()
            for copy in ahead if i == 0 else ():
                copy.start()
        columns = slice(start, start + TILE)
        raw_buf[i % 2, :, columns] = jnp.dot(
            q_buf[i].reshape(rows, lat),
            cache_buf[i, :, columns],
            preferred_element_type=jnp.float32,
        )

    scales = {}
    tails = {}

    def weight_piece(i, start):
        block = slice(start, start + BLOCK)
        limit = lengths[first + i] - (nq - 1) - me * tokens + (row + start) // heads
        raw = jnp.where(token < limit, raw_buf[i % 2, block, :], empty_mark)
        peak = jnp.max(raw, axis=1, keepdims=True)
        weights = jnp.exp2((raw - peak) * (score_scale * math.log2(math.e)))
        total = jnp.maximum(jnp.sum(weights, axis=1, keepdims=True), 1.0)
        low_buf[i % 2, block, :] = weights.astype(jnp.bfloat16)
        some = limit > 0
        scales[i, start] = jnp.where(some, 1.0 / total, 0.0)
        lse = jnp.where(some, peak * score_scale + jnp.log(total), empty_mark)
        part = start // 128
        spread = jnp.where(lane + part * 128 == row + start, lse, 0.0)
        tails[i, part] = tails.get((i, part), 0.0) + jnp.sum(spread, axis=0, keepdims=True)

    def value_piece(i, start):
        acc = lax.dot_general(
            low_buf[i % 2],
            cache_buf[i, start : start + TILE, :],
            (((1,), (1,)), ((), ())),
            preferred_element_type=jnp.float32,
        )
        for block in range(0, rows, BLOCK):
            acc_buf[i % 2, block : block + BLOCK, start : start + TILE] = acc[block : block + BLOCK] * scales[i, block]

    def out_piece(i):
        for mate, out in enumerate((keep, send)):
            for q in range(4):
                for j in range(nq):
                    source = pl.multiple_of(j * heads + group(me, q, mate, turn) * OWN, OWN)
                    to = ((q * count + i) * nq + j) * OWN
                    out[to : to + OWN, :] = acc_buf[i % 2, pl.ds(source, OWN), :]
        for part in range(rows // 128):
            for out in (keep, send):
                at = out.shape[0] - OWN + i
                out[at : at + 1, part * 128 : (part + 1) * 128] = tails[i, part]

    def pieces(stage, i):
        if not 0 <= i < count:
            return []
        if stage == 0:
            return [functools.partial(score_piece, i, t) for t in range(0, tokens, TILE)]
        if stage == 1:
            return [functools.partial(weight_piece, i, t) for t in range(0, rows, BLOCK)]
        return [functools.partial(value_piece, i, t) for t in range(0, kvr, TILE)] + [functools.partial(out_piece, i)]

    for i in range(count + 2):
        stages = [pieces(stage, i - stage) for stage in range(3)]
        marked = []
        for stage, own in enumerate(stages):
            marked += [((k + 0.5) / len(own), stage, k, piece) for k, piece in enumerate(own)]
        for _, _, _, piece in sorted(marked, key=lambda entry: entry[:3]):
            piece()
    for copy in ahead:
        copy.wait()


def attention(me, lengths, queries, cache, kvr, first, count, turn, ready, following, after, length):
    batch, nq, heads, lat = queries.shape
    tokens = cache.shape[2]
    rows = nq * heads
    out_rows = count * rows // 2 + OWN
    scratch = [
        pltpu.VMEM((2, rows, tokens), jnp.float32),
        pltpu.VMEM((2, rows, tokens), jnp.bfloat16),
        pltpu.VMEM((2, rows, kvr), jnp.float32),
        pltpu.SMEM((batch,), jnp.int32),
        pltpu.SemaphoreType.DMA,
        pltpu.SemaphoreType.DMA((max(following, 1), PIECES + 1)),
    ]
    if not ready:
        scratch += [
            pltpu.VMEM((count, nq, heads, lat), jnp.bfloat16),
            pltpu.VMEM((count, lat, tokens), jnp.bfloat16),
            pltpu.SemaphoreType.DMA((count, PIECES + 1)),
        ]
    out_shape = [jax.ShapeDtypeStruct((out_rows, kvr), jnp.float32)] * 2
    if following:
        out_shape += [
            jax.ShapeDtypeStruct((following, nq, heads, lat), jnp.bfloat16),
            jax.ShapeDtypeStruct((following, lat, tokens), jnp.bfloat16),
        ]
    return pl.pallas_call(
        functools.partial(attention_kernel, first, count, turn, len(ready) > 0, following, len(after)),
        in_specs=[SM, HB, HB, HB] + [VM] * len(ready) + [ANY] * len(after),
        out_specs=[VM] * len(out_shape),
        out_shape=out_shape,
        scratch_shapes=scratch,
        compiler_params=pltpu.CompilerParams(vmem_limit_bytes=24 * MIB),
        cost_estimate=declared(length),
    )(me, lengths, queries, cache, *ready, *after)


def merged(refs, shares):
    lanes = shares.shape[1]
    logs = [ref[ref.shape[0] - OWN :, :lanes] for ref in refs]
    largest = functools.reduce(jnp.maximum, logs)
    parts = [jnp.exp(log - largest) for log in logs]
    total = sum(parts[1:], parts[0])
    for k, part in enumerate(parts):
        shares[k] = (part / total).T
    return largest + jnp.log(total)


def merged_rows(refs, shares, me, heads, batch, q, b, j, turn):
    at = pl.ds(pl.multiple_of(j * heads + group(me, q, 0, turn) * OWN, OWN), OWN)
    source = ((q * batch + b) * (shares.shape[1] // heads) + j) * OWN
    rows = slice(source, source + OWN)
    terms_of = [shares[k, at, b : b + 1] * ref[rows, :] for k, ref in enumerate(refs)]
    return sum(terms_of[1:], terms_of[0])


def combine_kernel(places, pieces, batch, heads, turn, me_ref, keep_ref, got_ref, *refs):
    *outs, shares = refs[len(refs) - pieces - 1 :]
    lse = merged((keep_ref, got_ref), shares)
    lanes = shares.shape[1]
    size = batch * (lanes // heads) * OWN
    for q in range(places):
        side, at = divmod(q, places // pieces)
        for b in range(batch):
            for j in range(lanes // heads):
                to = at * size + (b * (lanes // heads) + j) * OWN
                outs[side][to : to + OWN, :] = merged_rows(
                    (keep_ref, got_ref), shares, me_ref[0], heads, batch, q, b, j, turn
                )
    for out in outs:
        out[out.shape[0] - OWN :, :] = jnp.zeros((OWN, out.shape[1]), jnp.float32)
        out[out.shape[0] - OWN :, :lanes] = lse


def combine(me, keep, got, places, pieces, batch, heads, lanes, turn, after, length):
    out_rows = (keep.shape[0] - OWN) // pieces + OWN
    return pl.pallas_call(
        functools.partial(combine_kernel, places, pieces, batch, heads, turn),
        in_specs=[SM, VM, VM] + [ANY] * len(after),
        out_specs=[VM] * pieces,
        out_shape=[jax.ShapeDtypeStruct((out_rows, keep.shape[1]), jnp.float32)] * pieces,
        scratch_shapes=[pltpu.VMEM((2, lanes, OWN), jnp.float32)],
        compiler_params=pltpu.CompilerParams(vmem_limit_bytes=16 * MIB),
        cost_estimate=declared(length),
    )(me, keep, got, *after)


def order_kernel(*refs):
    refs[-1][...] = jnp.zeros(refs[-1].shape, jnp.float32)


def order(after, length):
    return pl.pallas_call(
        order_kernel,
        in_specs=[ANY] * len(after),
        out_specs=VM,
        out_shape=jax.ShapeDtypeStruct((OWN, 128), jnp.float32),
        compiler_params=pltpu.CompilerParams(vmem_limit_bytes=MIB),
        cost_estimate=declared(length),
    )(*after)


def attend_rows(batch, heads, me, refs, shares, attended):
    merged(refs, shares)
    positions = shares.shape[1] // heads
    for b in range(batch):
        for j in range(positions):
            to = (b * positions + j) * OWN
            rows = merged_rows(refs, shares, me, heads, batch, 0, b, j, 0)
            for k in range(attended.shape[0]):
                attended[k, to : to + OWN, :] = rows[:, k * 128 : (k + 1) * 128]


def last_merge_kernel(batch, heads, count, me_ref, *refs):
    out_ref, shares = refs[-2:]
    attend_rows(batch, heads, me_ref[0], refs[:count], shares, out_ref)


def last_merge(me, arrays, batch, heads, lanes, after, length):
    rows, kvr = arrays[0].shape
    return pl.pallas_call(
        functools.partial(last_merge_kernel, batch, heads, len(arrays)),
        in_specs=[SM] + [VM] * len(arrays) + [ANY] * len(after),
        out_specs=VM,
        out_shape=jax.ShapeDtypeStruct((kvr // 128, rows - OWN, 128), jnp.float32),
        scratch_shapes=[pltpu.VMEM((len(arrays), lanes, OWN), jnp.float32)],
        compiler_params=pltpu.CompilerParams(vmem_limit_bytes=16 * MIB),
        cost_estimate=declared(length),
    )(me, *arrays, *after)


def heads_kernel(batch, heads, count, me_ref, *refs):
    early, refs = refs[: -count - 4], refs[-count - 4 :]
    arrays, (up_ref, out_ref, shares, attended) = refs[:count], refs[count:]
    attend_rows(batch, heads, me_ref[0], arrays, shares, attended)
    width = up_ref.shape[2]
    for i in range(OWN):
        own = [
            jnp.concatenate([ref[k, pl.ds(i, ref.shape[1] // OWN, stride=OWN), :] for k in range(ref.shape[0])], axis=1)
            for ref in (*early, attended)
        ]
        own = jnp.concatenate(own, axis=0).astype(jnp.bfloat16)
        head_out = jnp.dot(own, up_ref[i], preferred_element_type=jnp.float32)
        out_ref[:, i * width : (i + 1) * width] = head_out.astype(jnp.bfloat16)


def heads_out(me, early, arrays, batch, value_up, heads, lanes):
    rows, kvr = arrays[0].shape
    shape = (kvr // 128, rows - OWN, 128)
    places = sum(array.shape[1] for array in early) // OWN + shape[1] // OWN
    return pl.pallas_call(
        functools.partial(heads_kernel, batch, heads, len(arrays)),
        in_specs=[SM] + [VM] * (len(early) + len(arrays) + 1),
        out_specs=VM,
        out_shape=jax.ShapeDtypeStruct((places, OWN * value_up.shape[2]), jnp.bfloat16),
        scratch_shapes=[pltpu.VMEM((len(arrays), lanes, OWN), jnp.float32), pltpu.VMEM(shape, jnp.float32)],
        compiler_params=pltpu.CompilerParams(vmem_limit_bytes=16 * MIB),
        cost_estimate=declared(0),
    )(me, *early, *arrays, value_up)


def terms_kernel(mate, places, me_ref, heads_ref, weights_ref, *refs):
    out_ref = refs[-1]
    heads = heads_ref[...]
    width = out_ref.shape[2]
    for at, q in enumerate(places):
        start = pl.multiple_of(group(me_ref[0], q, mate, 0) * width, width)
        out_ref[at] = jnp.dot(heads, weights_ref[:, pl.ds(start, width)], preferred_element_type=jnp.float32)


def terms(me, heads, weights, mate, places, width, after, length):
    return pl.pallas_call(
        functools.partial(terms_kernel, mate, places),
        in_specs=[SM, VM, VM] + [ANY] * len(after),
        out_specs=VM,
        out_shape=jax.ShapeDtypeStruct((len(places), heads.shape[0], width), jnp.float32),
        compiler_params=pltpu.CompilerParams(vmem_limit_bytes=20 * MIB),
        cost_estimate=declared(length),
    )(me, heads, weights, *after)


def fold_kernel(own_ref, got_ref, *refs):
    for q, out in enumerate(refs[len(refs) - own_ref.shape[0] :]):
        out[...] = own_ref[q] + got_ref[q]


def fold(own, got, after):
    return pl.pallas_call(
        fold_kernel,
        in_specs=[VM, VM] + [ANY] * len(after),
        out_specs=[VM] * own.shape[0],
        out_shape=[jax.ShapeDtypeStruct(own.shape[1:], jnp.float32)] * own.shape[0],
        compiler_params=pltpu.CompilerParams(vmem_limit_bytes=8 * MIB),
        cost_estimate=declared(0),
    )(own, got, *after)


def finish_kernel(*refs):
    ins, out_ref = refs[:-1], refs[-1]
    batch, nq, _ = out_ref.shape
    total = ins[0][...]
    for ref in ins[1:]:
        total = total + ref[...]
    total = total.astype(jnp.bfloat16)
    for b in range(batch):
        out_ref[b] = total[b * nq : (b + 1) * nq, :]


def finish(terms_of, batch, nq):
    return pl.pallas_call(
        finish_kernel,
        in_specs=[VM] * len(terms_of),
        out_specs=VM,
        out_shape=jax.ShapeDtypeStruct((batch, nq, terms_of[0].shape[1]), jnp.bfloat16),
        compiler_params=pltpu.CompilerParams(vmem_limit_bytes=8 * MIB),
        cost_estimate=declared(0),
    )(*terms_of)


def local(n, queries, latent_cache, context_lengths, value_up, output_projection_rows):
    batch, nq, heads, _ = queries.shape
    kvr = value_up.shape[1]
    lanes = nq * heads
    me = lax.axis_index("seq").astype(jnp.int32).reshape(1)
    queries = pltpu.with_memory_space_constraint(queries, pltpu.HBM)
    cache = pltpu.with_memory_space_constraint(jnp.swapaxes(latent_cache, 1, 2), pltpu.HBM)
    lengths = pltpu.with_memory_space_constraint(context_lengths, pltpu.HBM)

    def swap(array, step, turn=0):
        return lax.ppermute(array, "seq", pairs_of(n, step, turn))

    keep, send, early = {}, {}, {}

    def arrived(p):
        turn = p & 1
        if len(send[p]) == 1:
            return [keep[p], swap(send[p][0], 2, turn)]
        second, first, both = send[p]
        return [keep[p], swap(first, 1, turn), swap(second, 2, turn), swap(both, 3, turn)]

    after, ready = (), ()
    for entry in ORDER.split():
        kind, p, length = entry[0], int(entry[1]), int(entry[3:])
        turn = p & 1
        if kind == "N":
            after = (order(after, length),)
        elif kind == "A":
            following = (*PARTS, 0)[p + 1]
            outs = attention(
                me, lengths, queries, cache, kvr, sum(PARTS[:p]), PARTS[p], turn, ready, following, after, length
            )
            keep[p], send[p], ready = outs[0], outs[1:2], outs[2:]
            after = (keep[p],)
        elif kind == "M":
            early[p] = last_merge(me, arrived(p), PARTS[p], heads, lanes, after, length)
            after = (early[p],)
        else:
            step = "CS".index(kind)
            pieces = 4 if kind == "C" and p in DIRECT else 2
            keep[p], *send[p] = combine(
                me,
                keep[p],
                swap(send[p][0], step, turn),
                4 >> step,
                pieces,
                PARTS[p],
                heads,
                lanes,
                turn,
                after,
                length,
            )
            after = (keep[p],)

    last = len(PARTS) - 1
    flat = heads_out(me, [early[p] for p in range(last)], arrived(last), PARTS[last], value_up, heads, lanes)
    width = output_projection_rows.shape[1] // n
    sums = {}
    after = ()
    for places in ((3, 2), (1, 0)):
        sent = terms(me, flat, output_projection_rows, 1, places, width, after, LAST[0])
        own = terms(me, flat, output_projection_rows, 0, places, width, (sent,), LAST[1])
        after = (order((own,), LAST[2]),) if LAST[2] and after else ()
        folded = fold(own, swap(sent, 0), after)
        sums.update(zip(places, folded))
        after = (folded[0],)
    return finish([sums[0], swap(sums[3], 3), swap(sums[2], 1), swap(sums[1], 2)], batch, nq)


def plain(queries, latent_cache, context_lengths, value_up, output_projection_rows):
    batch, nq = queries.shape[:2]
    kvr = value_up.shape[1]
    tokens = latent_cache.shape[1]
    scores = score_scale * jnp.einsum("bqhc,btc->bqht", queries, latent_cache, preferred_element_type=jnp.float32)
    position = lax.axis_index("seq") * tokens + jnp.arange(tokens, dtype=jnp.int32)
    limit = context_lengths[:, None] - (nq - 1) + jnp.arange(nq, dtype=jnp.int32)[None, :]
    visible = position[None, None, None, :] < limit[:, :, None, None]
    masked = jnp.where(visible, scores, empty_mark)
    peak = jnp.max(masked, axis=3)
    weights = jnp.where(visible, jnp.exp(masked - peak[..., None]), 0.0)
    total = jnp.maximum(jnp.sum(weights, axis=3), 1.0)
    values = jnp.einsum(
        "bqht,btc->bqhc", weights.astype(jnp.bfloat16), latent_cache[:, :, :kvr], preferred_element_type=jnp.float32
    )
    partials = lax.all_to_all((values / total[..., None])[None], "seq", split_axis=3, concat_axis=0, tiled=True)
    lse = lax.all_to_all((peak + jnp.log(total))[None], "seq", split_axis=3, concat_axis=0, tiled=True)
    shares = jnp.exp(lse - jnp.max(lse, axis=0)[None])
    attended = jnp.sum(shares[..., None] * partials, axis=0) / jnp.sum(shares, axis=0)[..., None]
    head_out = jnp.einsum(
        "bqhc,hcv->bqhv", attended.astype(jnp.bfloat16), value_up, preferred_element_type=jnp.float32
    )
    flat = head_out.astype(jnp.bfloat16).reshape(batch, nq, -1)
    term = jnp.einsum("msp,pc->msc", flat, output_projection_rows, preferred_element_type=jnp.float32)
    return lax.psum_scatter(term, "seq", scatter_dimension=2, tiled=True).astype(jnp.bfloat16)


def solution(mesh):
    n = mesh.shape["seq"]

    def body(queries, latent_cache, context_lengths, value_up, output_projection_rows):
        args = (queries, latent_cache, context_lengths, value_up, output_projection_rows)
        if n == 8 and value_up.shape[0] == OWN:
            return local(n, *args)
        return plain(*args)

    placed = (
        P("grp", None, None, None),
        P("grp", "seq", None),
        P("grp"),
        P("seq", None, None),
        P("seq", None),
    )
    return jax.shard_map(
        body, mesh=mesh, in_specs=placed, out_specs=P("grp", None, "seq"), check_vma=False
    )
```

```python
import functools
import math

import jax
import jax.numpy as jnp
from jax import lax
from jax.experimental import pallas as pl
from jax.experimental.pallas import tpu as pltpu
from jax.sharding import PartitionSpec as P

score_scale = 0.07216878364870323
empty_mark = -1e30
MIB = 1024 * 1024
PARTS = (2, 3, 3)
LAST = (50, 50, 0)
DIRECT = ()
ORDER = "A0:10 A1:10 C0:50 A2:10 C1:50 S0:50 C2:0 S1:0 S2:50 M0:5 M1:5"
BLOCK = 32
PIECES = 4
TILE = 256
OWN = 8
VM = pl.BlockSpec(memory_space=pltpu.VMEM)
SM = pl.BlockSpec(memory_space=pltpu.SMEM)
HB = pl.BlockSpec(memory_space=pltpu.HBM)
ANY = pl.BlockSpec(memory_space=pl.ANY)


def declared(length):
    return pl.CostEstimate(flops=length * 10**8 + 1, bytes_accessed=1, transcendentals=0)


def group(me, q, mate, turn):
    core = (me & 1) ^ mate ^ turn
    first = 2 + 2 * core
    return me ^ mate ^ ((q >> 1) * first + (q & 1) * (6 - first))


def pairs_of(n, step, turn):
    bits = ((1, 1), (2, 4), (4, 2), (6, 6))[step]
    return [(s, s ^ bits[(s & 1) ^ turn]) for s in range(n)]


def attention_kernel(first, count, turn, ready, following, after, me_ref, lengths_hbm, q_hbm, cache_hbm, *refs):
    q_buf, cache_buf = refs[:2] if ready else refs[-3:-1]
    refs = refs[2 * ready + after :]
    (keep, send), refs = refs[:2], refs[2:]
    targets, refs = refs[: 2 * (following > 0)], refs[2 * (following > 0) :]
    raw_buf, low_buf, acc_buf, lengths, length_sem, next_sems = refs[:6]
    nq, heads, lat = q_hbm.shape[1:]
    rows = nq * heads
    tokens = cache_hbm.shape[2]
    kvr = keep.shape[1]
    me = me_ref[0]
    length_copy = pltpu.make_async_copy(lengths_hbm, lengths, length_sem)
    length_copy.start()
    depth = lat // PIECES

    def copies(i, q_target, cache_target, sems):
        pieces = [slice(k * depth, (k + 1) * depth) for k in range(PIECES)]
        return [
            pltpu.make_async_copy(cache_hbm.at[first + i, piece], cache_target.at[piece], sems.at[k])
            for k, piece in enumerate(pieces)
        ] + [pltpu.make_async_copy(q_hbm.at[first + i], q_target, sems.at[PIECES])]

    ahead = [
        copy
        for i in range(following)
        for copy in copies(count + i, targets[0].at[i], targets[1].at[i], next_sems.at[i])
    ]
    fetches = []
    if not ready:
        fetches = [copies(i, q_buf.at[i], cache_buf.at[i], refs[-1].at[i]) for i in range(count)]
    for copy in sum(fetches, []) or ahead:
        copy.start()
    row = lax.broadcasted_iota(jnp.int32, (BLOCK, 1), 0)
    token = lax.broadcasted_iota(jnp.int32, (BLOCK, tokens), 1)
    lane = lax.broadcasted_iota(jnp.int32, (BLOCK, 128), 1)
    for out in (keep, send):
        out[out.shape[0] - OWN :, :] = jnp.zeros((OWN, kvr), jnp.float32)
    length_copy.wait()

    def score_piece(i, start):
        if fetches and start == 0:
            for copy in fetches[i]:
                copy.wait()
            for copy in ahead if i == 0 else ():
                copy.start()
        columns = slice(start, start + TILE)
        raw_buf[i % 2, :, columns] = jnp.dot(
            q_buf[i].reshape(rows, lat),
            cache_buf[i, :, columns],
            preferred_element_type=jnp.float32,
        )

    scales = {}
    tails = {}

    def weight_piece(i, start):
        block = slice(start, start + BLOCK)
        limit = lengths[first + i] - (nq - 1) - me * tokens + (row + start) // heads
        raw = jnp.where(token < limit, raw_buf[i % 2, block, :], empty_mark)
        peak = jnp.max(raw, axis=1, keepdims=True)
        weights = jnp.exp2((raw - peak) * (score_scale * math.log2(math.e)))
        total = jnp.maximum(jnp.sum(weights, axis=1, keepdims=True), 1.0)
        low_buf[i % 2, block, :] = weights.astype(jnp.bfloat16)
        some = limit > 0
        scales[i, start] = jnp.where(some, 1.0 / total, 0.0)
        lse = jnp.where(some, peak * score_scale + jnp.log(total), empty_mark)
        part = start // 128
        spread = jnp.where(lane + part * 128 == row + start, lse, 0.0)
        tails[i, part] = tails.get((i, part), 0.0) + jnp.sum(spread, axis=0, keepdims=True)

    def value_piece(i, start):
        acc = lax.dot_general(
            low_buf[i % 2],
            cache_buf[i, start : start + TILE, :],
            (((1,), (1,)), ((), ())),
            preferred_element_type=jnp.float32,
        )
        for block in range(0, rows, BLOCK):
            acc_buf[i % 2, block : block + BLOCK, start : start + TILE] = acc[block : block + BLOCK] * scales[i, block]

    def out_piece(i):
        for mate, out in enumerate((keep, send)):
            for q in range(4):
                for j in range(nq):
                    source = pl.multiple_of(j * heads + group(me, q, mate, turn) * OWN, OWN)
                    to = ((q * count + i) * nq + j) * OWN
                    out[to : to + OWN, :] = acc_buf[i % 2, pl.ds(source, OWN), :]
        for part in range(rows // 128):
            for out in (keep, send):
                at = out.shape[0] - OWN + i
                out[at : at + 1, part * 128 : (part + 1) * 128] = tails[i, part]

    def pieces(stage, i):
        if not 0 <= i < count:
            return []
        if stage == 0:
            return [functools.partial(score_piece, i, t) for t in range(0, tokens, TILE)]
        if stage == 1:
            return [functools.partial(weight_piece, i, t) for t in range(0, rows, BLOCK)]
        return [functools.partial(value_piece, i, t) for t in range(0, kvr, TILE)] + [functools.partial(out_piece, i)]

    for i in range(count + 2):
        stages = [pieces(stage, i - stage) for stage in range(3)]
        marked = []
        for stage, own in enumerate(stages):
            marked += [((k + 0.5) / len(own), stage, k, piece) for k, piece in enumerate(own)]
        for _, _, _, piece in sorted(marked, key=lambda entry: entry[:3]):
            piece()
    for copy in ahead:
        copy.wait()


def attention(me, lengths, queries, cache, kvr, first, count, turn, ready, following, after, length):
    batch, nq, heads, lat = queries.shape
    tokens = cache.shape[2]
    rows = nq * heads
    out_rows = count * rows // 2 + OWN
    scratch = [
        pltpu.VMEM((2, rows, tokens), jnp.float32),
        pltpu.VMEM((2, rows, tokens), jnp.bfloat16),
        pltpu.VMEM((2, rows, kvr), jnp.float32),
        pltpu.SMEM((batch,), jnp.int32),
        pltpu.SemaphoreType.DMA,
        pltpu.SemaphoreType.DMA((max(following, 1), PIECES + 1)),
    ]
    if not ready:
        scratch += [
            pltpu.VMEM((count, nq, heads, lat), jnp.bfloat16),
            pltpu.VMEM((count, lat, tokens), jnp.bfloat16),
            pltpu.SemaphoreType.DMA((count, PIECES + 1)),
        ]
    out_shape = [jax.ShapeDtypeStruct((out_rows, kvr), jnp.float32)] * 2
    if following:
        out_shape += [
            jax.ShapeDtypeStruct((following, nq, heads, lat), jnp.bfloat16),
            jax.ShapeDtypeStruct((following, lat, tokens), jnp.bfloat16),
        ]
    return pl.pallas_call(
        functools.partial(attention_kernel, first, count, turn, len(ready) > 0, following, len(after)),
        in_specs=[SM, HB, HB, HB] + [VM] * len(ready) + [ANY] * len(after),
        out_specs=[VM] * len(out_shape),
        out_shape=out_shape,
        scratch_shapes=scratch,
        compiler_params=pltpu.CompilerParams(vmem_limit_bytes=24 * MIB),
        cost_estimate=declared(length),
    )(me, lengths, queries, cache, *ready, *after)


def merged(refs, shares):
    lanes = shares.shape[1]
    logs = [ref[ref.shape[0] - OWN :, :lanes] for ref in refs]
    largest = functools.reduce(jnp.maximum, logs)
    parts = [jnp.exp(log - largest) for log in logs]
    total = sum(parts[1:], parts[0])
    for k, part in enumerate(parts):
        shares[k] = (part / total).T
    return largest + jnp.log(total)


def merged_rows(refs, shares, me, heads, batch, q, b, j, turn):
    at = pl.ds(pl.multiple_of(j * heads + group(me, q, 0, turn) * OWN, OWN), OWN)
    source = ((q * batch + b) * (shares.shape[1] // heads) + j) * OWN
    rows = slice(source, source + OWN)
    terms_of = [shares[k, at, b : b + 1] * ref[rows, :] for k, ref in enumerate(refs)]
    return sum(terms_of[1:], terms_of[0])


def combine_kernel(places, pieces, batch, heads, turn, me_ref, keep_ref, got_ref, *refs):
    *outs, shares = refs[len(refs) - pieces - 1 :]
    lse = merged((keep_ref, got_ref), shares)
    lanes = shares.shape[1]
    size = batch * (lanes // heads) * OWN
    for q in range(places):
        side, at = divmod(q, places // pieces)
        for b in range(batch):
            for j in range(lanes // heads):
                to = at * size + (b * (lanes // heads) + j) * OWN
                outs[side][to : to + OWN, :] = merged_rows(
                    (keep_ref, got_ref), shares, me_ref[0], heads, batch, q, b, j, turn
                )
    for out in outs:
        out[out.shape[0] - OWN :, :] = jnp.zeros((OWN, out.shape[1]), jnp.float32)
        out[out.shape[0] - OWN :, :lanes] = lse


def combine(me, keep, got, places, pieces, batch, heads, lanes, turn, after, length):
    out_rows = (keep.shape[0] - OWN) // pieces + OWN
    return pl.pallas_call(
        functools.partial(combine_kernel, places, pieces, batch, heads, turn),
        in_specs=[SM, VM, VM] + [ANY] * len(after),
        out_specs=[VM] * pieces,
        out_shape=[jax.ShapeDtypeStruct((out_rows, keep.shape[1]), jnp.float32)] * pieces,
        scratch_shapes=[pltpu.VMEM((2, lanes, OWN), jnp.float32)],
        compiler_params=pltpu.CompilerParams(vmem_limit_bytes=16 * MIB),
        cost_estimate=declared(length),
    )(me, keep, got, *after)


def order_kernel(*refs):
    refs[-1][...] = jnp.zeros(refs[-1].shape, jnp.float32)


def order(after, length):
    return pl.pallas_call(
        order_kernel,
        in_specs=[ANY] * len(after),
        out_specs=VM,
        out_shape=jax.ShapeDtypeStruct((OWN, 128), jnp.float32),
        compiler_params=pltpu.CompilerParams(vmem_limit_bytes=MIB),
        cost_estimate=declared(length),
    )(*after)


def attend_rows(batch, heads, me, refs, shares, attended):
    merged(refs, shares)
    positions = shares.shape[1] // heads
    for b in range(batch):
        for j in range(positions):
            to = (b * positions + j) * OWN
            rows = merged_rows(refs, shares, me, heads, batch, 0, b, j, 0)
            for k in range(attended.shape[0]):
                attended[k, to : to + OWN, :] = rows[:, k * 128 : (k + 1) * 128]


def last_merge_kernel(batch, heads, count, me_ref, *refs):
    out_ref, shares = refs[-2:]
    attend_rows(batch, heads, me_ref[0], refs[:count], shares, out_ref)


def last_merge(me, arrays, batch, heads, lanes, after, length):
    rows, kvr = arrays[0].shape
    return pl.pallas_call(
        functools.partial(last_merge_kernel, batch, heads, len(arrays)),
        in_specs=[SM] + [VM] * len(arrays) + [ANY] * len(after),
        out_specs=VM,
        out_shape=jax.ShapeDtypeStruct((kvr // 128, rows - OWN, 128), jnp.float32),
        scratch_shapes=[pltpu.VMEM((len(arrays), lanes, OWN), jnp.float32)],
        compiler_params=pltpu.CompilerParams(vmem_limit_bytes=16 * MIB),
        cost_estimate=declared(length),
    )(me, *arrays, *after)


def heads_kernel(batch, heads, count, me_ref, *refs):
    early, refs = refs[: -count - 4], refs[-count - 4 :]
    arrays, (up_ref, out_ref, shares, attended) = refs[:count], refs[count:]
    attend_rows(batch, heads, me_ref[0], arrays, shares, attended)
    width = up_ref.shape[2]
    for i in range(OWN):
        own = [
            jnp.concatenate([ref[k, pl.ds(i, ref.shape[1] // OWN, stride=OWN), :] for k in range(ref.shape[0])], axis=1)
            for ref in (*early, attended)
        ]
        own = jnp.concatenate(own, axis=0).astype(jnp.bfloat16)
        head_out = jnp.dot(own, up_ref[i], preferred_element_type=jnp.float32)
        out_ref[:, i * width : (i + 1) * width] = head_out.astype(jnp.bfloat16)


def heads_out(me, early, arrays, batch, value_up, heads, lanes):
    rows, kvr = arrays[0].shape
    shape = (kvr // 128, rows - OWN, 128)
    places = sum(array.shape[1] for array in early) // OWN + shape[1] // OWN
    return pl.pallas_call(
        functools.partial(heads_kernel, batch, heads, len(arrays)),
        in_specs=[SM] + [VM] * (len(early) + len(arrays) + 1),
        out_specs=VM,
        out_shape=jax.ShapeDtypeStruct((places, OWN * value_up.shape[2]), jnp.bfloat16),
        scratch_shapes=[pltpu.VMEM((len(arrays), lanes, OWN), jnp.float32), pltpu.VMEM(shape, jnp.float32)],
        compiler_params=pltpu.CompilerParams(vmem_limit_bytes=16 * MIB),
        cost_estimate=declared(0),
    )(me, *early, *arrays, value_up)


def terms_kernel(mate, places, me_ref, heads_ref, weights_ref, *refs):
    out_ref = refs[-1]
    heads = heads_ref[...]
    width = out_ref.shape[2]
    for at, q in enumerate(places):
        start = pl.multiple_of(group(me_ref[0], q, mate, 0) * width, width)
        out_ref[at] = jnp.dot(heads, weights_ref[:, pl.ds(start, width)], preferred_element_type=jnp.float32)


def terms(me, heads, weights, mate, places, width, after, length):
    return pl.pallas_call(
        functools.partial(terms_kernel, mate, places),
        in_specs=[SM, VM, VM] + [ANY] * len(after),
        out_specs=VM,
        out_shape=jax.ShapeDtypeStruct((len(places), heads.shape[0], width), jnp.float32),
        compiler_params=pltpu.CompilerParams(vmem_limit_bytes=20 * MIB),
        cost_estimate=declared(length),
    )(me, heads, weights, *after)


def fold_kernel(own_ref, got_ref, *refs):
    for q, out in enumerate(refs[len(refs) - own_ref.shape[0] :]):
        out[...] = own_ref[q] + got_ref[q]


def fold(own, got, after):
    return pl.pallas_call(
        fold_kernel,
        in_specs=[VM, VM] + [ANY] * len(after),
        out_specs=[VM] * own.shape[0],
        out_shape=[jax.ShapeDtypeStruct(own.shape[1:], jnp.float32)] * own.shape[0],
        compiler_params=pltpu.CompilerParams(vmem_limit_bytes=8 * MIB),
        cost_estimate=declared(0),
    )(own, got, *after)


def finish_kernel(*refs):
    ins, out_ref = refs[:-1], refs[-1]
    batch, nq, _ = out_ref.shape
    total = ins[0][...]
    for ref in ins[1:]:
        total = total + ref[...]
    total = total.astype(jnp.bfloat16)
    for b in range(batch):
        out_ref[b] = total[b * nq : (b + 1) * nq, :]


def finish(terms_of, batch, nq):
    return pl.pallas_call(
        finish_kernel,
        in_specs=[VM] * len(terms_of),
        out_specs=VM,
        out_shape=jax.ShapeDtypeStruct((batch, nq, terms_of[0].shape[1]), jnp.bfloat16),
        compiler_params=pltpu.CompilerParams(vmem_limit_bytes=8 * MIB),
        cost_estimate=declared(0),
    )(*terms_of)


def local(n, queries, latent_cache, context_lengths, value_up, output_projection_rows):
    batch, nq, heads, _ = queries.shape
    kvr = value_up.shape[1]
    lanes = nq * heads
    me = lax.axis_index("seq").astype(jnp.int32).reshape(1)
    queries = pltpu.with_memory_space_constraint(queries, pltpu.HBM)
    cache = pltpu.with_memory_space_constraint(jnp.swapaxes(latent_cache, 1, 2), pltpu.HBM)
    lengths = pltpu.with_memory_space_constraint(context_lengths, pltpu.HBM)

    def swap(array, step, turn=0):
        return lax.ppermute(array, "seq", pairs_of(n, step, turn))

    keep, send, early = {}, {}, {}

    def arrived(p):
        turn = p & 1
        if len(send[p]) == 1:
            return [keep[p], swap(send[p][0], 2, turn)]
        second, first, both = send[p]
        return [keep[p], swap(first, 1, turn), swap(second, 2, turn), swap(both, 3, turn)]

    after, ready = (), ()
    for entry in ORDER.split():
        kind, p, length = entry[0], int(entry[1]), int(entry[3:])
        turn = p & 1
        if kind == "N":
            after = (order(after, length),)
        elif kind == "A":
            following = (*PARTS, 0)[p + 1]
            outs = attention(
                me, lengths, queries, cache, kvr, sum(PARTS[:p]), PARTS[p], turn, ready, following, after, length
            )
            keep[p], send[p], ready = outs[0], outs[1:2], outs[2:]
            after = (keep[p],)
        elif kind == "M":
            early[p] = last_merge(me, arrived(p), PARTS[p], heads, lanes, after, length)
            after = (early[p],)
        else:
            step = "CS".index(kind)
            pieces = 4 if kind == "C" and p in DIRECT else 2
            keep[p], *send[p] = combine(
                me,
                keep[p],
                swap(send[p][0], step, turn),
                4 >> step,
                pieces,
                PARTS[p],
                heads,
                lanes,
                turn,
                after,
                length,
            )
            after = (keep[p],)

    last = len(PARTS) - 1
    flat = heads_out(me, [early[p] for p in range(last)], arrived(last), PARTS[last], value_up, heads, lanes)
    width = output_projection_rows.shape[1] // n
    sums = {}
    after = ()
    for places in ((3, 2), (1, 0)):
        sent = terms(me, flat, output_projection_rows, 1, places, width, after, LAST[0])
        own = terms(me, flat, output_projection_rows, 0, places, width, (sent,), LAST[1])
        after = (order((own,), LAST[2]),) if LAST[2] and after else ()
        folded = fold(own, swap(sent, 0), after)
        sums.update(zip(places, folded))
        after = (folded[0],)
    return finish([sums[0], swap(sums[3], 3), swap(sums[2], 1), swap(sums[1], 2)], batch, nq)


def plain(queries, latent_cache, context_lengths, value_up, output_projection_rows):
    batch, nq = queries.shape[:2]
    kvr = value_up.shape[1]
    tokens = latent_cache.shape[1]
    scores = score_scale * jnp.einsum("bqhc,btc->bqht", queries, latent_cache, preferred_element_type=jnp.float32)
    position = lax.axis_index("seq") * tokens + jnp.arange(tokens, dtype=jnp.int32)
    limit = context_lengths[:, None] - (nq - 1) + jnp.arange(nq, dtype=jnp.int32)[None, :]
    visible = position[None, None, None, :] < limit[:, :, None, None]
    masked = jnp.where(visible, scores, empty_mark)
    peak = jnp.max(masked, axis=3)
    weights = jnp.where(visible, jnp.exp(masked - peak[..., None]), 0.0)
    total = jnp.maximum(jnp.sum(weights, axis=3), 1.0)
    values = jnp.einsum(
        "bqht,btc->bqhc", weights.astype(jnp.bfloat16), latent_cache[:, :, :kvr], preferred_element_type=jnp.float32
    )
    partials = lax.all_to_all((values / total[..., None])[None], "seq", split_axis=3, concat_axis=0, tiled=True)
    lse = lax.all_to_all((peak + jnp.log(total))[None], "seq", split_axis=3, concat_axis=0, tiled=True)
    shares = jnp.exp(lse - jnp.max(lse, axis=0)[None])
    attended = jnp.sum(shares[..., None] * partials, axis=0) / jnp.sum(shares, axis=0)[..., None]
    head_out = jnp.einsum(
        "bqhc,hcv->bqhv", attended.astype(jnp.bfloat16), value_up, preferred_element_type=jnp.float32
    )
    flat = head_out.astype(jnp.bfloat16).reshape(batch, nq, -1)
    term = jnp.einsum("msp,pc->msc", flat, output_projection_rows, preferred_element_type=jnp.float32)
    return lax.psum_scatter(term, "seq", scatter_dimension=2, tiled=True).astype(jnp.bfloat16)


def solution(mesh):
    n = mesh.shape["seq"]

    def body(queries, latent_cache, context_lengths, value_up, output_projection_rows):
        args = (queries, latent_cache, context_lengths, value_up, output_projection_rows)
        if n == 8 and value_up.shape[0] == OWN:
            return local(n, *args)
        return plain(*args)

    placed = (
        P("grp", None, None, None),
        P("grp", "seq", None),
        P("grp"),
        P("seq", None, None),
        P("seq", None),
    )
    return jax.shard_map(
        body, mesh=mesh, in_specs=placed, out_specs=P("grp", None, "seq"), check_vma=False
    )
```

```python
import functools
import math

import jax
import jax.numpy as jnp
from jax import lax
from jax.experimental import pallas as pl
from jax.experimental.pallas import tpu as pltpu
from jax.sharding import PartitionSpec as P

score_scale = 0.07216878364870323
empty_mark = -1e30
MIB = 1024 * 1024
PARTS = (2, 2, 2, 2)
LAST = (50, 50, 0)
DIRECT = ()
ORDER = "A0:10 A1:10 C0:50 A2:10 C1:50 A3:10 C2:50 S0:50 C3:0 S1:0 S2:0 S3:50 M0:5 M1:5 M2:5"
BLOCK = 32
PIECES = 4
TILE = 256
OWN = 8
VM = pl.BlockSpec(memory_space=pltpu.VMEM)
SM = pl.BlockSpec(memory_space=pltpu.SMEM)
HB = pl.BlockSpec(memory_space=pltpu.HBM)
ANY = pl.BlockSpec(memory_space=pl.ANY)


def declared(length):
    return pl.CostEstimate(flops=length * 10**8 + 1, bytes_accessed=1, transcendentals=0)


def group(me, q, mate, turn):
    core = (me & 1) ^ mate ^ turn
    first = 2 + 2 * core
    return me ^ mate ^ ((q >> 1) * first + (q & 1) * (6 - first))


def pairs_of(n, step, turn):
    bits = ((1, 1), (2, 4), (4, 2), (6, 6))[step]
    return [(s, s ^ bits[(s & 1) ^ turn]) for s in range(n)]


def attention_kernel(first, count, turn, ready, following, after, me_ref, lengths_hbm, q_hbm, cache_hbm, *refs):
    q_buf, cache_buf = refs[:2] if ready else refs[-3:-1]
    refs = refs[2 * ready + after :]
    (keep, send), refs = refs[:2], refs[2:]
    targets, refs = refs[: 2 * (following > 0)], refs[2 * (following > 0) :]
    raw_buf, low_buf, acc_buf, lengths, length_sem, next_sems = refs[:6]
    nq, heads, lat = q_hbm.shape[1:]
    rows = nq * heads
    tokens = cache_hbm.shape[2]
    kvr = acc_buf.shape[2]
    me = me_ref[0]
    length_copy = pltpu.make_async_copy(lengths_hbm, lengths, length_sem)
    length_copy.start()
    depth = lat // PIECES

    def copies(i, q_target, cache_target, sems):
        pieces = [slice(k * depth, (k + 1) * depth) for k in range(PIECES)]
        return [
            pltpu.make_async_copy(cache_hbm.at[first + i, piece], cache_target.at[piece], sems.at[k])
            for k, piece in enumerate(pieces)
        ] + [pltpu.make_async_copy(q_hbm.at[first + i], q_target, sems.at[PIECES])]

    ahead = [
        copy
        for i in range(following)
        for copy in copies(count + i, targets[0].at[i], targets[1].at[i], next_sems.at[i])
    ]
    fetches = []
    if not ready:
        fetches = [copies(i, q_buf.at[i], cache_buf.at[i], refs[-1].at[i]) for i in range(count)]
    for copy in sum(fetches, []) or ahead:
        copy.start()
    row = lax.broadcasted_iota(jnp.int32, (BLOCK, 1), 0)
    token = lax.broadcasted_iota(jnp.int32, (BLOCK, tokens), 1)
    lane = lax.broadcasted_iota(jnp.int32, (BLOCK, 128), 1)
    for out in (keep, send):
        out[out.shape[0] - OWN :, :] = jnp.zeros((OWN, 128), jnp.float32)
    length_copy.wait()

    def score_piece(i, start):
        if fetches and start == 0:
            for copy in fetches[i]:
                copy.wait()
            for copy in ahead if i == 0 else ():
                copy.start()
        columns = slice(start, start + TILE)
        raw_buf[i % 2, :, columns] = jnp.dot(
            q_buf[i].reshape(rows, lat),
            cache_buf[i, :, columns],
            preferred_element_type=jnp.float32,
        )

    scales = {}
    tails = {}

    def weight_piece(i, start):
        block = slice(start, start + BLOCK)
        limit = lengths[first + i] - (nq - 1) - me * tokens + (row + start) // heads
        raw = jnp.where(token < limit, raw_buf[i % 2, block, :], empty_mark)
        peak = jnp.max(raw, axis=1, keepdims=True)
        weights = jnp.exp2((raw - peak) * (score_scale * math.log2(math.e)))
        total = jnp.maximum(jnp.sum(weights, axis=1, keepdims=True), 1.0)
        low_buf[i % 2, block, :] = weights.astype(jnp.bfloat16)
        some = limit > 0
        scales[i, start] = jnp.where(some, 1.0 / total, 0.0)
        lse = jnp.where(some, peak * score_scale + jnp.log(total), empty_mark)
        part = start // 128
        spread = jnp.where(lane + part * 128 == row + start, lse, 0.0)
        tails[i, part] = tails.get((i, part), 0.0) + jnp.sum(spread, axis=0, keepdims=True)

    def value_piece(i, start):
        acc = lax.dot_general(
            low_buf[i % 2],
            cache_buf[i, start : start + TILE, :],
            (((1,), (1,)), ((), ())),
            preferred_element_type=jnp.float32,
        )
        for block in range(0, rows, BLOCK):
            acc_buf[i % 2, block : block + BLOCK, start : start + TILE] = acc[block : block + BLOCK] * scales[i, block]

    def out_piece(i):
        for mate, out in enumerate((keep, send)):
            for q in range(4):
                for j in range(nq):
                    source = pl.multiple_of(j * heads + group(me, q, mate, turn) * OWN, OWN)
                    to = ((q * count + i) * nq + j) * OWN
                    for k in range(kvr // 128):
                        at = k * 4 * count * nq * OWN + to
                        out[at : at + OWN, :] = acc_buf[i % 2, pl.ds(source, OWN), k * 128 : (k + 1) * 128]
        for part in range(rows // 128):
            for out in (keep, send):
                at = out.shape[0] - OWN + i * (rows // 128) + part
                out[at : at + 1, :] = tails[i, part]

    def pieces(stage, i):
        if not 0 <= i < count:
            return []
        if stage == 0:
            return [functools.partial(score_piece, i, t) for t in range(0, tokens, TILE)]
        if stage == 1:
            return [functools.partial(weight_piece, i, t) for t in range(0, rows, BLOCK)]
        return [functools.partial(value_piece, i, t) for t in range(0, kvr, TILE)] + [functools.partial(out_piece, i)]

    for i in range(count + 2):
        stages = [pieces(stage, i - stage) for stage in range(3)]
        marked = []
        for stage, own in enumerate(stages):
            marked += [((k + 0.5) / len(own), stage, k, piece) for k, piece in enumerate(own)]
        for _, _, _, piece in sorted(marked, key=lambda entry: entry[:3]):
            piece()
    for copy in ahead:
        copy.wait()


def attention(me, lengths, queries, cache, kvr, first, count, turn, ready, following, after, length):
    batch, nq, heads, lat = queries.shape
    tokens = cache.shape[2]
    rows = nq * heads
    out_rows = kvr // 128 * count * rows // 2 + OWN
    scratch = [
        pltpu.VMEM((2, rows, tokens), jnp.float32),
        pltpu.VMEM((2, rows, tokens), jnp.bfloat16),
        pltpu.VMEM((2, rows, kvr), jnp.float32),
        pltpu.SMEM((batch,), jnp.int32),
        pltpu.SemaphoreType.DMA,
        pltpu.SemaphoreType.DMA((max(following, 1), PIECES + 1)),
    ]
    if not ready:
        scratch += [
            pltpu.VMEM((count, nq, heads, lat), jnp.bfloat16),
            pltpu.VMEM((count, lat, tokens), jnp.bfloat16),
            pltpu.SemaphoreType.DMA((count, PIECES + 1)),
        ]
    out_shape = [jax.ShapeDtypeStruct((out_rows, 128), jnp.float32)] * 2
    if following:
        out_shape += [
            jax.ShapeDtypeStruct((following, nq, heads, lat), jnp.bfloat16),
            jax.ShapeDtypeStruct((following, lat, tokens), jnp.bfloat16),
        ]
    return pl.pallas_call(
        functools.partial(attention_kernel, first, count, turn, len(ready) > 0, following, len(after)),
        in_specs=[SM, HB, HB, HB] + [VM] * len(ready) + [ANY] * len(after),
        out_specs=[VM] * len(out_shape),
        out_shape=out_shape,
        scratch_shapes=scratch,
        compiler_params=pltpu.CompilerParams(vmem_limit_bytes=24 * MIB),
        cost_estimate=declared(length),
    )(me, lengths, queries, cache, *ready, *after)


def merged(refs, shares):
    logs = [ref[ref.shape[0] - OWN :, :] for ref in refs]
    largest = functools.reduce(jnp.maximum, logs)
    parts = [jnp.exp(log - largest) for log in logs]
    total = sum(parts[1:], parts[0])
    for k, part in enumerate(parts):
        shares[k] = (part / total).T
    return largest + jnp.log(total)


def merged_rows(refs, shares, me, sizes, places, q, b, j, turn):
    batch, nq, heads = sizes
    line, within = divmod(b * nq * heads + j * heads, 128)
    at = pl.ds(pl.multiple_of(within + group(me, q, 0, turn) * OWN, OWN), OWN)
    columns = [shares[k, at, line : line + 1] for k in range(len(refs))]
    height = places * batch * nq * OWN
    source = ((q * batch + b) * nq + j) * OWN
    for start in range(source, refs[0].shape[0] - OWN, height):
        terms_of = [column * ref[start : start + OWN, :] for column, ref in zip(columns, refs)]
        yield sum(terms_of[1:], terms_of[0])


def combine_kernel(places, pieces, sizes, turn, me_ref, keep_ref, got_ref, *refs):
    *outs, shares = refs[len(refs) - pieces - 1 :]
    lse = merged((keep_ref, got_ref), shares)
    batch, nq, _ = sizes
    size = batch * nq * OWN
    for q in range(places):
        side, at = divmod(q, places // pieces)
        for b in range(batch):
            for j in range(nq):
                blocks = merged_rows((keep_ref, got_ref), shares, me_ref[0], sizes, places, q, b, j, turn)
                for k, block in enumerate(blocks):
                    to = (k * (places // pieces) + at) * size + (b * nq + j) * OWN
                    outs[side][to : to + OWN, :] = block
    for out in outs:
        out[out.shape[0] - OWN :, :] = lse


def combine(me, keep, got, places, pieces, sizes, turn, after, length):
    out_rows = (keep.shape[0] - OWN) // pieces + OWN
    return pl.pallas_call(
        functools.partial(combine_kernel, places, pieces, sizes, turn),
        in_specs=[SM, VM, VM] + [ANY] * len(after),
        out_specs=[VM] * pieces,
        out_shape=[jax.ShapeDtypeStruct((out_rows, 128), jnp.float32)] * pieces,
        scratch_shapes=[pltpu.VMEM((2, 128, OWN), jnp.float32)],
        compiler_params=pltpu.CompilerParams(vmem_limit_bytes=16 * MIB),
        cost_estimate=declared(length),
    )(me, keep, got, *after)


def order_kernel(*refs):
    refs[-1][...] = jnp.zeros(refs[-1].shape, jnp.float32)


def order(after, length):
    return pl.pallas_call(
        order_kernel,
        in_specs=[ANY] * len(after),
        out_specs=VM,
        out_shape=jax.ShapeDtypeStruct((OWN, 128), jnp.float32),
        compiler_params=pltpu.CompilerParams(vmem_limit_bytes=MIB),
        cost_estimate=declared(length),
    )(*after)


def attend_rows(sizes, me, refs, shares, attended):
    merged(refs, shares)
    batch, nq, _ = sizes
    for b in range(batch):
        for j in range(nq):
            to = (b * nq + j) * OWN
            for k, block in enumerate(merged_rows(refs, shares, me, sizes, 1, 0, b, j, 0)):
                attended[k, to : to + OWN, :] = block


def attended_shape(array, sizes):
    rows = sizes[0] * sizes[1] * OWN
    return ((array.shape[0] - OWN) // rows, rows, 128)


def last_merge_kernel(sizes, count, me_ref, *refs):
    out_ref, shares = refs[-2:]
    attend_rows(sizes, me_ref[0], refs[:count], shares, out_ref)


def last_merge(me, arrays, sizes, after, length):
    return pl.pallas_call(
        functools.partial(last_merge_kernel, sizes, len(arrays)),
        in_specs=[SM] + [VM] * len(arrays) + [ANY] * len(after),
        out_specs=VM,
        out_shape=jax.ShapeDtypeStruct(attended_shape(arrays[0], sizes), jnp.float32),
        scratch_shapes=[pltpu.VMEM((len(arrays), 128, OWN), jnp.float32)],
        compiler_params=pltpu.CompilerParams(vmem_limit_bytes=16 * MIB),
        cost_estimate=declared(length),
    )(me, *arrays, *after)


def heads_kernel(sizes, count, me_ref, *refs):
    early, refs = refs[: -count - 4], refs[-count - 4 :]
    arrays, (up_ref, out_ref, shares, attended) = refs[:count], refs[count:]
    attend_rows(sizes, me_ref[0], arrays, shares, attended)
    width = up_ref.shape[2]
    for i in range(OWN):
        own = [
            jnp.concatenate([ref[k, pl.ds(i, ref.shape[1] // OWN, stride=OWN), :] for k in range(ref.shape[0])], axis=1)
            for ref in (*early, attended)
        ]
        own = jnp.concatenate(own, axis=0).astype(jnp.bfloat16)
        head_out = jnp.dot(own, up_ref[i], preferred_element_type=jnp.float32)
        out_ref[:, i * width : (i + 1) * width] = head_out.astype(jnp.bfloat16)


def heads_out(me, early, arrays, sizes, value_up):
    shape = attended_shape(arrays[0], sizes)
    places = sum(array.shape[1] for array in early) // OWN + shape[1] // OWN
    return pl.pallas_call(
        functools.partial(heads_kernel, sizes, len(arrays)),
        in_specs=[SM] + [VM] * (len(early) + len(arrays) + 1),
        out_specs=VM,
        out_shape=jax.ShapeDtypeStruct((places, OWN * value_up.shape[2]), jnp.bfloat16),
        scratch_shapes=[pltpu.VMEM((len(arrays), 128, OWN), jnp.float32), pltpu.VMEM(shape, jnp.float32)],
        compiler_params=pltpu.CompilerParams(vmem_limit_bytes=16 * MIB),
        cost_estimate=declared(0),
    )(me, *early, *arrays, value_up)


def terms_kernel(mate, places, me_ref, heads_ref, weights_ref, *refs):
    out_ref = refs[-1]
    heads = heads_ref[...]
    width = out_ref.shape[2]
    for at, q in enumerate(places):
        start = pl.multiple_of(group(me_ref[0], q, mate, 0) * width, width)
        out_ref[at] = jnp.dot(heads, weights_ref[:, pl.ds(start, width)], preferred_element_type=jnp.float32)


def terms(me, heads, weights, mate, places, width, after, length):
    return pl.pallas_call(
        functools.partial(terms_kernel, mate, places),
        in_specs=[SM, VM, VM] + [ANY] * len(after),
        out_specs=VM,
        out_shape=jax.ShapeDtypeStruct((len(places), heads.shape[0], width), jnp.float32),
        compiler_params=pltpu.CompilerParams(vmem_limit_bytes=20 * MIB),
        cost_estimate=declared(length),
    )(me, heads, weights, *after)


def fold_kernel(own_ref, got_ref, *refs):
    for q, out in enumerate(refs[len(refs) - own_ref.shape[0] :]):
        out[...] = own_ref[q] + got_ref[q]


def fold(own, got, after):
    return pl.pallas_call(
        fold_kernel,
        in_specs=[VM, VM] + [ANY] * len(after),
        out_specs=[VM] * own.shape[0],
        out_shape=[jax.ShapeDtypeStruct(own.shape[1:], jnp.float32)] * own.shape[0],
        compiler_params=pltpu.CompilerParams(vmem_limit_bytes=8 * MIB),
        cost_estimate=declared(0),
    )(own, got, *after)


def finish_kernel(*refs):
    ins, out_ref = refs[:-1], refs[-1]
    batch, nq, _ = out_ref.shape
    total = ins[0][...]
    for ref in ins[1:]:
        total = total + ref[...]
    total = total.astype(jnp.bfloat16)
    for b in range(batch):
        out_ref[b] = total[b * nq : (b + 1) * nq, :]


def finish(terms_of, batch, nq):
    return pl.pallas_call(
        finish_kernel,
        in_specs=[VM] * len(terms_of),
        out_specs=VM,
        out_shape=jax.ShapeDtypeStruct((batch, nq, terms_of[0].shape[1]), jnp.bfloat16),
        compiler_params=pltpu.CompilerParams(vmem_limit_bytes=8 * MIB),
        cost_estimate=declared(0),
    )(*terms_of)


def local(n, queries, latent_cache, context_lengths, value_up, output_projection_rows):
    batch, nq, heads, _ = queries.shape
    kvr = value_up.shape[1]
    me = lax.axis_index("seq").astype(jnp.int32).reshape(1)
    queries = pltpu.with_memory_space_constraint(queries, pltpu.HBM)
    cache = pltpu.with_memory_space_constraint(jnp.swapaxes(latent_cache, 1, 2), pltpu.HBM)
    lengths = pltpu.with_memory_space_constraint(context_lengths, pltpu.HBM)

    def swap(array, step, turn=0):
        return lax.ppermute(array, "seq", pairs_of(n, step, turn))

    keep, send, early = {}, {}, {}

    def arrived(p):
        turn = p & 1
        if len(send[p]) == 1:
            return [keep[p], swap(send[p][0], 2, turn)]
        second, first, both = send[p]
        return [keep[p], swap(first, 1, turn), swap(second, 2, turn), swap(both, 3, turn)]

    after, ready = (), ()
    for entry in ORDER.split():
        kind, p, length = entry[0], int(entry[1]), int(entry[3:])
        turn, sizes = p & 1, (PARTS[p], nq, heads)
        if kind == "N":
            after = (order(after, length),)
        elif kind == "A":
            following = (*PARTS, 0)[p + 1]
            outs = attention(
                me, lengths, queries, cache, kvr, sum(PARTS[:p]), PARTS[p], turn, ready, following, after, length
            )
            keep[p], send[p], ready = outs[0], outs[1:2], outs[2:]
            after = (keep[p],)
        elif kind == "M":
            early[p] = last_merge(me, arrived(p), sizes, after, length)
            after = (early[p],)
        else:
            step = "CS".index(kind)
            pieces = 4 if kind == "C" and p in DIRECT else 2
            keep[p], *send[p] = combine(
                me,
                keep[p],
                swap(send[p][0], step, turn),
                4 >> step,
                pieces,
                sizes,
                turn,
                after,
                length,
            )
            after = (keep[p],)

    last = len(PARTS) - 1
    flat = heads_out(me, [early[p] for p in range(last)], arrived(last), (PARTS[last], nq, heads), value_up)
    width = output_projection_rows.shape[1] // n
    sums = {}
    after = ()
    for places in ((3, 2), (1, 0)):
        sent = terms(me, flat, output_projection_rows, 1, places, width, after, LAST[0])
        own = terms(me, flat, output_projection_rows, 0, places, width, (sent,), LAST[1])
        after = (order((own,), LAST[2]),) if LAST[2] and after else ()
        folded = fold(own, swap(sent, 0), after)
        sums.update(zip(places, folded))
        after = (folded[0],)
    return finish([sums[0], swap(sums[3], 3), swap(sums[2], 1), swap(sums[1], 2)], batch, nq)


def plain(queries, latent_cache, context_lengths, value_up, output_projection_rows):
    batch, nq = queries.shape[:2]
    kvr = value_up.shape[1]
    tokens = latent_cache.shape[1]
    scores = score_scale * jnp.einsum("bqhc,btc->bqht", queries, latent_cache, preferred_element_type=jnp.float32)
    position = lax.axis_index("seq") * tokens + jnp.arange(tokens, dtype=jnp.int32)
    limit = context_lengths[:, None] - (nq - 1) + jnp.arange(nq, dtype=jnp.int32)[None, :]
    visible = position[None, None, None, :] < limit[:, :, None, None]
    masked = jnp.where(visible, scores, empty_mark)
    peak = jnp.max(masked, axis=3)
    weights = jnp.where(visible, jnp.exp(masked - peak[..., None]), 0.0)
    total = jnp.maximum(jnp.sum(weights, axis=3), 1.0)
    values = jnp.einsum(
        "bqht,btc->bqhc", weights.astype(jnp.bfloat16), latent_cache[:, :, :kvr], preferred_element_type=jnp.float32
    )
    partials = lax.all_to_all((values / total[..., None])[None], "seq", split_axis=3, concat_axis=0, tiled=True)
    lse = lax.all_to_all((peak + jnp.log(total))[None], "seq", split_axis=3, concat_axis=0, tiled=True)
    shares = jnp.exp(lse - jnp.max(lse, axis=0)[None])
    attended = jnp.sum(shares[..., None] * partials, axis=0) / jnp.sum(shares, axis=0)[..., None]
    head_out = jnp.einsum(
        "bqhc,hcv->bqhv", attended.astype(jnp.bfloat16), value_up, preferred_element_type=jnp.float32
    )
    flat = head_out.astype(jnp.bfloat16).reshape(batch, nq, -1)
    term = jnp.einsum("msp,pc->msc", flat, output_projection_rows, preferred_element_type=jnp.float32)
    return lax.psum_scatter(term, "seq", scatter_dimension=2, tiled=True).astype(jnp.bfloat16)


def solution(mesh):
    n = mesh.shape["seq"]

    def body(queries, latent_cache, context_lengths, value_up, output_projection_rows):
        args = (queries, latent_cache, context_lengths, value_up, output_projection_rows)
        if n == 8 and value_up.shape[0] == OWN:
            return local(n, *args)
        return plain(*args)

    placed = (
        P("grp", None, None, None),
        P("grp", "seq", None),
        P("grp"),
        P("seq", None, None),
        P("seq", None),
    )
    return jax.shard_map(
        body, mesh=mesh, in_specs=placed, out_specs=P("grp", None, "seq"), check_vma=False
    )
```

```python
import functools
import math

import jax
import jax.numpy as jnp
from jax import lax
from jax.experimental import pallas as pl
from jax.experimental.pallas import tpu as pltpu
from jax.sharding import PartitionSpec as P

score_scale = 0.07216878364870323
empty_mark = -1e30
MIB = 1024 * 1024
PARTS = (3, 2, 2, 1)
LAST = (50, 50, 0)
DIRECT = ()
ORDER = "A0:10 A1:10 C0:50 A2:10 C1:50 A3:10 C2:50 S0:50 C3:0 S1:0 S2:0 S3:50 M0:5 M1:5 M2:5"
BLOCK = 32
PIECES = 4
TILE = 256
OWN = 8
VM = pl.BlockSpec(memory_space=pltpu.VMEM)
SM = pl.BlockSpec(memory_space=pltpu.SMEM)
HB = pl.BlockSpec(memory_space=pltpu.HBM)
ANY = pl.BlockSpec(memory_space=pl.ANY)


def declared(length):
    return pl.CostEstimate(flops=length * 10**8 + 1, bytes_accessed=1, transcendentals=0)


def group(me, q, mate, turn):
    core = (me & 1) ^ mate ^ turn
    first = 2 + 2 * core
    return me ^ mate ^ ((q >> 1) * first + (q & 1) * (6 - first))


def pairs_of(n, step, turn):
    bits = ((1, 1), (2, 4), (4, 2), (6, 6))[step]
    return [(s, s ^ bits[(s & 1) ^ turn]) for s in range(n)]


def attention_kernel(first, count, turn, ready, following, after, me_ref, lengths_hbm, q_hbm, cache_hbm, *refs):
    q_buf, cache_buf = refs[:2] if ready else refs[-3:-1]
    refs = refs[2 * ready + after :]
    (keep, send), refs = refs[:2], refs[2:]
    targets, refs = refs[: 2 * (following > 0)], refs[2 * (following > 0) :]
    raw_buf, low_buf, acc_buf, lengths, length_sem, next_sems = refs[:6]
    nq, heads, lat = q_hbm.shape[1:]
    rows = nq * heads
    tokens = cache_hbm.shape[2]
    kvr = acc_buf.shape[2]
    me = me_ref[0]
    length_copy = pltpu.make_async_copy(lengths_hbm, lengths, length_sem)
    length_copy.start()
    depth = lat // PIECES

    def copies(i, q_target, cache_target, sems):
        pieces = [slice(k * depth, (k + 1) * depth) for k in range(PIECES)]
        return [
            pltpu.make_async_copy(cache_hbm.at[first + i, piece], cache_target.at[piece], sems.at[k])
            for k, piece in enumerate(pieces)
        ] + [pltpu.make_async_copy(q_hbm.at[first + i], q_target, sems.at[PIECES])]

    ahead = [
        copy
        for i in range(following)
        for copy in copies(count + i, targets[0].at[i], targets[1].at[i], next_sems.at[i])
    ]
    fetches = []
    if not ready:
        fetches = [copies(i, q_buf.at[i], cache_buf.at[i], refs[-1].at[i]) for i in range(count)]
    for copy in sum(fetches, []) or ahead:
        copy.start()
    row = lax.broadcasted_iota(jnp.int32, (BLOCK, 1), 0)
    token = lax.broadcasted_iota(jnp.int32, (BLOCK, tokens), 1)
    lane = lax.broadcasted_iota(jnp.int32, (BLOCK, 128), 1)
    for out in (keep, send):
        out[out.shape[0] - OWN :, :] = jnp.zeros((OWN, 128), jnp.float32)
    length_copy.wait()

    def score_piece(i, start):
        if fetches and start == 0:
            for copy in fetches[i]:
                copy.wait()
            for copy in ahead if i == 0 else ():
                copy.start()
        columns = slice(start, start + TILE)
        raw_buf[i % 2, :, columns] = jnp.dot(
            q_buf[i].reshape(rows, lat),
            cache_buf[i, :, columns],
            preferred_element_type=jnp.float32,
        )

    scales = {}
    tails = {}

    def weight_piece(i, start):
        block = slice(start, start + BLOCK)
        limit = lengths[first + i] - (nq - 1) - me * tokens + (row + start) // heads
        raw = jnp.where(token < limit, raw_buf[i % 2, block, :], empty_mark)
        peak = jnp.max(raw, axis=1, keepdims=True)
        weights = jnp.exp2((raw - peak) * (score_scale * math.log2(math.e)))
        total = jnp.maximum(jnp.sum(weights, axis=1, keepdims=True), 1.0)
        low_buf[i % 2, block, :] = weights.astype(jnp.bfloat16)
        some = limit > 0
        scales[i, start] = jnp.where(some, 1.0 / total, 0.0)
        lse = jnp.where(some, peak * score_scale + jnp.log(total), empty_mark)
        part = start // 128
        spread = jnp.where(lane + part * 128 == row + start, lse, 0.0)
        tails[i, part] = tails.get((i, part), 0.0) + jnp.sum(spread, axis=0, keepdims=True)

    def value_piece(i, start):
        acc = lax.dot_general(
            low_buf[i % 2],
            cache_buf[i, start : start + TILE, :],
            (((1,), (1,)), ((), ())),
            preferred_element_type=jnp.float32,
        )
        for block in range(0, rows, BLOCK):
            acc_buf[i % 2, block : block + BLOCK, start : start + TILE] = acc[block : block + BLOCK] * scales[i, block]

    def out_piece(i):
        for mate, out in enumerate((keep, send)):
            for q in range(4):
                for j in range(nq):
                    source = pl.multiple_of(j * heads + group(me, q, mate, turn) * OWN, OWN)
                    to = ((q * count + i) * nq + j) * OWN
                    for k in range(kvr // 128):
                        at = k * 4 * count * nq * OWN + to
                        out[at : at + OWN, :] = acc_buf[i % 2, pl.ds(source, OWN), k * 128 : (k + 1) * 128]
        for part in range(rows // 128):
            for out in (keep, send):
                at = out.shape[0] - OWN + i * (rows // 128) + part
                out[at : at + 1, :] = tails[i, part]

    def pieces(stage, i):
        if not 0 <= i < count:
            return []
        if stage == 0:
            return [functools.partial(score_piece, i, t) for t in range(0, tokens, TILE)]
        if stage == 1:
            return [functools.partial(weight_piece, i, t) for t in range(0, rows, BLOCK)]
        return [functools.partial(value_piece, i, t) for t in range(0, kvr, TILE)] + [functools.partial(out_piece, i)]

    for i in range(count + 2):
        stages = [pieces(stage, i - stage) for stage in range(3)]
        marked = []
        for stage, own in enumerate(stages):
            marked += [((k + 0.5) / len(own), stage, k, piece) for k, piece in enumerate(own)]
        for _, _, _, piece in sorted(marked, key=lambda entry: entry[:3]):
            piece()
    for copy in ahead:
        copy.wait()


def attention(me, lengths, queries, cache, kvr, first, count, turn, ready, following, after, length):
    batch, nq, heads, lat = queries.shape
    tokens = cache.shape[2]
    rows = nq * heads
    out_rows = kvr // 128 * count * rows // 2 + OWN
    scratch = [
        pltpu.VMEM((2, rows, tokens), jnp.float32),
        pltpu.VMEM((2, rows, tokens), jnp.bfloat16),
        pltpu.VMEM((2, rows, kvr), jnp.float32),
        pltpu.SMEM((batch,), jnp.int32),
        pltpu.SemaphoreType.DMA,
        pltpu.SemaphoreType.DMA((max(following, 1), PIECES + 1)),
    ]
    if not ready:
        scratch += [
            pltpu.VMEM((count, nq, heads, lat), jnp.bfloat16),
            pltpu.VMEM((count, lat, tokens), jnp.bfloat16),
            pltpu.SemaphoreType.DMA((count, PIECES + 1)),
        ]
    out_shape = [jax.ShapeDtypeStruct((out_rows, 128), jnp.float32)] * 2
    if following:
        out_shape += [
            jax.ShapeDtypeStruct((following, nq, heads, lat), jnp.bfloat16),
            jax.ShapeDtypeStruct((following, lat, tokens), jnp.bfloat16),
        ]
    return pl.pallas_call(
        functools.partial(attention_kernel, first, count, turn, len(ready) > 0, following, len(after)),
        in_specs=[SM, HB, HB, HB] + [VM] * len(ready) + [ANY] * len(after),
        out_specs=[VM] * len(out_shape),
        out_shape=out_shape,
        scratch_shapes=scratch,
        compiler_params=pltpu.CompilerParams(vmem_limit_bytes=24 * MIB),
        cost_estimate=declared(length),
    )(me, lengths, queries, cache, *ready, *after)


def merged(refs, shares):
    logs = [ref[ref.shape[0] - OWN :, :] for ref in refs]
    largest = functools.reduce(jnp.maximum, logs)
    parts = [jnp.exp(log - largest) for log in logs]
    total = sum(parts[1:], parts[0])
    for k, part in enumerate(parts):
        shares[k] = (part / total).T
    return largest + jnp.log(total)


def merged_rows(refs, shares, me, sizes, places, q, b, j, turn):
    batch, nq, heads = sizes
    line, within = divmod(b * nq * heads + j * heads, 128)
    at = pl.ds(pl.multiple_of(within + group(me, q, 0, turn) * OWN, OWN), OWN)
    columns = [shares[k, at, line : line + 1] for k in range(len(refs))]
    height = places * batch * nq * OWN
    source = ((q * batch + b) * nq + j) * OWN
    for start in range(source, refs[0].shape[0] - OWN, height):
        terms_of = [column * ref[start : start + OWN, :] for column, ref in zip(columns, refs)]
        yield sum(terms_of[1:], terms_of[0])


def combine_kernel(places, pieces, sizes, turn, me_ref, keep_ref, got_ref, *refs):
    *outs, shares = refs[len(refs) - pieces - 1 :]
    lse = merged((keep_ref, got_ref), shares)
    batch, nq, _ = sizes
    size = batch * nq * OWN
    for q in range(places):
        side, at = divmod(q, places // pieces)
        for b in range(batch):
            for j in range(nq):
                blocks = merged_rows((keep_ref, got_ref), shares, me_ref[0], sizes, places, q, b, j, turn)
                for k, block in enumerate(blocks):
                    to = (k * (places // pieces) + at) * size + (b * nq + j) * OWN
                    outs[side][to : to + OWN, :] = block
    for out in outs:
        out[out.shape[0] - OWN :, :] = lse


def combine(me, keep, got, places, pieces, sizes, turn, after, length):
    out_rows = (keep.shape[0] - OWN) // pieces + OWN
    return pl.pallas_call(
        functools.partial(combine_kernel, places, pieces, sizes, turn),
        in_specs=[SM, VM, VM] + [ANY] * len(after),
        out_specs=[VM] * pieces,
        out_shape=[jax.ShapeDtypeStruct((out_rows, 128), jnp.float32)] * pieces,
        scratch_shapes=[pltpu.VMEM((2, 128, OWN), jnp.float32)],
        compiler_params=pltpu.CompilerParams(vmem_limit_bytes=16 * MIB),
        cost_estimate=declared(length),
    )(me, keep, got, *after)


def order_kernel(*refs):
    refs[-1][...] = jnp.zeros(refs[-1].shape, jnp.float32)


def order(after, length):
    return pl.pallas_call(
        order_kernel,
        in_specs=[ANY] * len(after),
        out_specs=VM,
        out_shape=jax.ShapeDtypeStruct((OWN, 128), jnp.float32),
        compiler_params=pltpu.CompilerParams(vmem_limit_bytes=MIB),
        cost_estimate=declared(length),
    )(*after)


def attend_rows(sizes, me, refs, shares, attended):
    merged(refs, shares)
    batch, nq, _ = sizes
    for b in range(batch):
        for j in range(nq):
            to = (b * nq + j) * OWN
            for k, block in enumerate(merged_rows(refs, shares, me, sizes, 1, 0, b, j, 0)):
                attended[k, to : to + OWN, :] = block


def attended_shape(array, sizes):
    rows = sizes[0] * sizes[1] * OWN
    return ((array.shape[0] - OWN) // rows, rows, 128)


def last_merge_kernel(sizes, count, me_ref, *refs):
    out_ref, shares = refs[-2:]
    attend_rows(sizes, me_ref[0], refs[:count], shares, out_ref)


def last_merge(me, arrays, sizes, after, length):
    return pl.pallas_call(
        functools.partial(last_merge_kernel, sizes, len(arrays)),
        in_specs=[SM] + [VM] * len(arrays) + [ANY] * len(after),
        out_specs=VM,
        out_shape=jax.ShapeDtypeStruct(attended_shape(arrays[0], sizes), jnp.float32),
        scratch_shapes=[pltpu.VMEM((len(arrays), 128, OWN), jnp.float32)],
        compiler_params=pltpu.CompilerParams(vmem_limit_bytes=16 * MIB),
        cost_estimate=declared(length),
    )(me, *arrays, *after)


def heads_kernel(sizes, count, me_ref, *refs):
    early, refs = refs[: -count - 4], refs[-count - 4 :]
    arrays, (up_ref, out_ref, shares, attended) = refs[:count], refs[count:]
    attend_rows(sizes, me_ref[0], arrays, shares, attended)
    width = up_ref.shape[2]
    for i in range(OWN):
        own = [
            jnp.concatenate([ref[k, pl.ds(i, ref.shape[1] // OWN, stride=OWN), :] for k in range(ref.shape[0])], axis=1)
            for ref in (*early, attended)
        ]
        own = jnp.concatenate(own, axis=0).astype(jnp.bfloat16)
        head_out = jnp.dot(own, up_ref[i], preferred_element_type=jnp.float32)
        out_ref[:, i * width : (i + 1) * width] = head_out.astype(jnp.bfloat16)


def heads_out(me, early, arrays, sizes, value_up):
    shape = attended_shape(arrays[0], sizes)
    places = sum(array.shape[1] for array in early) // OWN + shape[1] // OWN
    return pl.pallas_call(
        functools.partial(heads_kernel, sizes, len(arrays)),
        in_specs=[SM] + [VM] * (len(early) + len(arrays) + 1),
        out_specs=VM,
        out_shape=jax.ShapeDtypeStruct((places, OWN * value_up.shape[2]), jnp.bfloat16),
        scratch_shapes=[pltpu.VMEM((len(arrays), 128, OWN), jnp.float32), pltpu.VMEM(shape, jnp.float32)],
        compiler_params=pltpu.CompilerParams(vmem_limit_bytes=16 * MIB),
        cost_estimate=declared(0),
    )(me, *early, *arrays, value_up)


def terms_kernel(mate, places, me_ref, heads_ref, weights_ref, *refs):
    out_ref = refs[-1]
    heads = heads_ref[...]
    width = out_ref.shape[2]
    for at, q in enumerate(places):
        start = pl.multiple_of(group(me_ref[0], q, mate, 0) * width, width)
        out_ref[at] = jnp.dot(heads, weights_ref[:, pl.ds(start, width)], preferred_element_type=jnp.float32)


def terms(me, heads, weights, mate, places, width, after, length):
    return pl.pallas_call(
        functools.partial(terms_kernel, mate, places),
        in_specs=[SM, VM, VM] + [ANY] * len(after),
        out_specs=VM,
        out_shape=jax.ShapeDtypeStruct((len(places), heads.shape[0], width), jnp.float32),
        compiler_params=pltpu.CompilerParams(vmem_limit_bytes=20 * MIB),
        cost_estimate=declared(length),
    )(me, heads, weights, *after)


def fold_kernel(own_ref, got_ref, *refs):
    for q, out in enumerate(refs[len(refs) - own_ref.shape[0] :]):
        out[...] = own_ref[q] + got_ref[q]


def fold(own, got, after):
    return pl.pallas_call(
        fold_kernel,
        in_specs=[VM, VM] + [ANY] * len(after),
        out_specs=[VM] * own.shape[0],
        out_shape=[jax.ShapeDtypeStruct(own.shape[1:], jnp.float32)] * own.shape[0],
        compiler_params=pltpu.CompilerParams(vmem_limit_bytes=8 * MIB),
        cost_estimate=declared(0),
    )(own, got, *after)


def finish_kernel(*refs):
    ins, out_ref = refs[:-1], refs[-1]
    batch, nq, _ = out_ref.shape
    total = ins[0][...]
    for ref in ins[1:]:
        total = total + ref[...]
    total = total.astype(jnp.bfloat16)
    for b in range(batch):
        out_ref[b] = total[b * nq : (b + 1) * nq, :]


def finish(terms_of, batch, nq):
    return pl.pallas_call(
        finish_kernel,
        in_specs=[VM] * len(terms_of),
        out_specs=VM,
        out_shape=jax.ShapeDtypeStruct((batch, nq, terms_of[0].shape[1]), jnp.bfloat16),
        compiler_params=pltpu.CompilerParams(vmem_limit_bytes=8 * MIB),
        cost_estimate=declared(0),
    )(*terms_of)


def local(n, queries, latent_cache, context_lengths, value_up, output_projection_rows):
    batch, nq, heads, _ = queries.shape
    kvr = value_up.shape[1]
    me = lax.axis_index("seq").astype(jnp.int32).reshape(1)
    queries = pltpu.with_memory_space_constraint(queries, pltpu.HBM)
    cache = pltpu.with_memory_space_constraint(jnp.swapaxes(latent_cache, 1, 2), pltpu.HBM)
    lengths = pltpu.with_memory_space_constraint(context_lengths, pltpu.HBM)

    def swap(array, step, turn=0):
        return lax.ppermute(array, "seq", pairs_of(n, step, turn))

    keep, send, early = {}, {}, {}

    def arrived(p):
        turn = p & 1
        if len(send[p]) == 1:
            return [keep[p], swap(send[p][0], 2, turn)]
        second, first, both = send[p]
        return [keep[p], swap(first, 1, turn), swap(second, 2, turn), swap(both, 3, turn)]

    after, ready = (), ()
    for entry in ORDER.split():
        kind, p, length = entry[0], int(entry[1]), int(entry[3:])
        turn, sizes = p & 1, (PARTS[p], nq, heads)
        if kind == "N":
            after = (order(after, length),)
        elif kind == "A":
            following = (*PARTS, 0)[p + 1]
            outs = attention(
                me, lengths, queries, cache, kvr, sum(PARTS[:p]), PARTS[p], turn, ready, following, after, length
            )
            keep[p], send[p], ready = outs[0], outs[1:2], outs[2:]
            after = (keep[p],)
        elif kind == "M":
            early[p] = last_merge(me, arrived(p), sizes, after, length)
            after = (early[p],)
        else:
            step = "CS".index(kind)
            pieces = 4 if kind == "C" and p in DIRECT else 2
            keep[p], *send[p] = combine(
                me,
                keep[p],
                swap(send[p][0], step, turn),
                4 >> step,
                pieces,
                sizes,
                turn,
                after,
                length,
            )
            after = (keep[p],)

    last = len(PARTS) - 1
    flat = heads_out(me, [early[p] for p in range(last)], arrived(last), (PARTS[last], nq, heads), value_up)
    width = output_projection_rows.shape[1] // n
    sums = {}
    after = ()
    for places in ((3, 2), (1, 0)):
        sent = terms(me, flat, output_projection_rows, 1, places, width, after, LAST[0])
        own = terms(me, flat, output_projection_rows, 0, places, width, (sent,), LAST[1])
        after = (order((own,), LAST[2]),) if LAST[2] and after else ()
        folded = fold(own, swap(sent, 0), after)
        sums.update(zip(places, folded))
        after = (folded[0],)
    return finish([sums[0], swap(sums[3], 3), swap(sums[2], 1), swap(sums[1], 2)], batch, nq)


def plain(queries, latent_cache, context_lengths, value_up, output_projection_rows):
    batch, nq = queries.shape[:2]
    kvr = value_up.shape[1]
    tokens = latent_cache.shape[1]
    scores = score_scale * jnp.einsum("bqhc,btc->bqht", queries, latent_cache, preferred_element_type=jnp.float32)
    position = lax.axis_index("seq") * tokens + jnp.arange(tokens, dtype=jnp.int32)
    limit = context_lengths[:, None] - (nq - 1) + jnp.arange(nq, dtype=jnp.int32)[None, :]
    visible = position[None, None, None, :] < limit[:, :, None, None]
    masked = jnp.where(visible, scores, empty_mark)
    peak = jnp.max(masked, axis=3)
    weights = jnp.where(visible, jnp.exp(masked - peak[..., None]), 0.0)
    total = jnp.maximum(jnp.sum(weights, axis=3), 1.0)
    values = jnp.einsum(
        "bqht,btc->bqhc", weights.astype(jnp.bfloat16), latent_cache[:, :, :kvr], preferred_element_type=jnp.float32
    )
    partials = lax.all_to_all((values / total[..., None])[None], "seq", split_axis=3, concat_axis=0, tiled=True)
    lse = lax.all_to_all((peak + jnp.log(total))[None], "seq", split_axis=3, concat_axis=0, tiled=True)
    shares = jnp.exp(lse - jnp.max(lse, axis=0)[None])
    attended = jnp.sum(shares[..., None] * partials, axis=0) / jnp.sum(shares, axis=0)[..., None]
    head_out = jnp.einsum(
        "bqhc,hcv->bqhv", attended.astype(jnp.bfloat16), value_up, preferred_element_type=jnp.float32
    )
    flat = head_out.astype(jnp.bfloat16).reshape(batch, nq, -1)
    term = jnp.einsum("msp,pc->msc", flat, output_projection_rows, preferred_element_type=jnp.float32)
    return lax.psum_scatter(term, "seq", scatter_dimension=2, tiled=True).astype(jnp.bfloat16)


def solution(mesh):
    n = mesh.shape["seq"]

    def body(queries, latent_cache, context_lengths, value_up, output_projection_rows):
        args = (queries, latent_cache, context_lengths, value_up, output_projection_rows)
        if n == 8 and value_up.shape[0] == OWN:
            return local(n, *args)
        return plain(*args)

    placed = (
        P("grp", None, None, None),
        P("grp", "seq", None),
        P("grp"),
        P("seq", None, None),
        P("seq", None),
    )
    return jax.shard_map(
        body, mesh=mesh, in_specs=placed, out_specs=P("grp", None, "seq"), check_vma=False
    )
```

```python
import functools
import math

import jax
import jax.numpy as jnp
from jax import lax
from jax.experimental import pallas as pl
from jax.experimental.pallas import tpu as pltpu
from jax.sharding import PartitionSpec as P

score_scale = 0.07216878364870323
empty_mark = -1e30
MIB = 1024 * 1024
PARTS = (2, 2, 2, 2)
LAST = (50, 50, 0)
DIRECT = ()
ORDER = "A0:10 A1:10 C0:50 A2:10 C1:50 A3:10 C2:50 S0:50 C3:50 S1:20 S2:20 S3:50 M0:5 M1:5 M2:5"
BLOCK = 32
PIECES = 4
TILE = 256
OWN = 8
VM = pl.BlockSpec(memory_space=pltpu.VMEM)
SM = pl.BlockSpec(memory_space=pltpu.SMEM)
HB = pl.BlockSpec(memory_space=pltpu.HBM)
ANY = pl.BlockSpec(memory_space=pl.ANY)


def declared(length):
    return pl.CostEstimate(flops=length * 10**8 + 1, bytes_accessed=1, transcendentals=0)


def group(me, q, mate, turn):
    core = (me & 1) ^ mate ^ turn
    first = 2 + 2 * core
    return me ^ mate ^ ((q >> 1) * first + (q & 1) * (6 - first))


def pairs_of(n, step, turn):
    bits = ((1, 1), (2, 4), (4, 2), (6, 6))[step]
    return [(s, s ^ bits[(s & 1) ^ turn]) for s in range(n)]


def attention_kernel(first, count, turn, ready, following, after, me_ref, lengths_hbm, q_hbm, cache_hbm, *refs):
    q_buf, cache_buf = refs[:2] if ready else refs[-3:-1]
    refs = refs[2 * ready + after :]
    (keep, send), refs = refs[:2], refs[2:]
    targets, refs = refs[: 2 * (following > 0)], refs[2 * (following > 0) :]
    raw_buf, low_buf, acc_buf, lengths, length_sem, next_sems = refs[:6]
    nq, heads, lat = q_hbm.shape[1:]
    rows = nq * heads
    tokens = cache_hbm.shape[2]
    kvr = acc_buf.shape[2]
    me = me_ref[0]
    length_copy = pltpu.make_async_copy(lengths_hbm, lengths, length_sem)
    length_copy.start()
    depth = lat // PIECES

    def copies(i, q_target, cache_target, sems):
        pieces = [slice(k * depth, (k + 1) * depth) for k in range(PIECES)]
        return [
            pltpu.make_async_copy(cache_hbm.at[first + i, piece], cache_target.at[piece], sems.at[k])
            for k, piece in enumerate(pieces)
        ] + [pltpu.make_async_copy(q_hbm.at[first + i], q_target, sems.at[PIECES])]

    ahead = [
        copy
        for i in range(following)
        for copy in copies(count + i, targets[0].at[i], targets[1].at[i], next_sems.at[i])
    ]
    fetches = []
    if not ready:
        fetches = [copies(i, q_buf.at[i], cache_buf.at[i], refs[-1].at[i]) for i in range(count)]
    for copy in sum(fetches, []) or ahead:
        copy.start()
    row = lax.broadcasted_iota(jnp.int32, (BLOCK, 1), 0)
    token = lax.broadcasted_iota(jnp.int32, (BLOCK, tokens), 1)
    lane = lax.broadcasted_iota(jnp.int32, (BLOCK, 128), 1)
    for out in (keep, send):
        out[out.shape[0] - OWN :, :] = jnp.zeros((OWN, 128), jnp.float32)
    length_copy.wait()

    def score_piece(i, start):
        if fetches and start == 0:
            for copy in fetches[i]:
                copy.wait()
            for copy in ahead if i == 0 else ():
                copy.start()
        columns = slice(start, start + TILE)
        raw_buf[i % 2, :, columns] = jnp.dot(
            q_buf[i].reshape(rows, lat),
            cache_buf[i, :, columns],
            preferred_element_type=jnp.float32,
        )

    scales = {}
    tails = {}

    def weight_piece(i, start):
        block = slice(start, start + BLOCK)
        limit = lengths[first + i] - (nq - 1) - me * tokens + (row + start) // heads
        raw = jnp.where(token < limit, raw_buf[i % 2, block, :], empty_mark)
        peak = jnp.max(raw, axis=1, keepdims=True)
        weights = jnp.exp2((raw - peak) * (score_scale * math.log2(math.e)))
        total = jnp.maximum(jnp.sum(weights, axis=1, keepdims=True), 1.0)
        low_buf[i % 2, block, :] = weights.astype(jnp.bfloat16)
        some = limit > 0
        scales[i, start] = jnp.where(some, 1.0 / total, 0.0)
        lse = jnp.where(some, peak * score_scale + jnp.log(total), empty_mark)
        part = start // 128
        spread = jnp.where(lane + part * 128 == row + start, lse, 0.0)
        tails[i, part] = tails.get((i, part), 0.0) + jnp.sum(spread, axis=0, keepdims=True)

    def value_piece(i, start):
        acc = lax.dot_general(
            low_buf[i % 2],
            cache_buf[i, start : start + TILE, :],
            (((1,), (1,)), ((), ())),
            preferred_element_type=jnp.float32,
        )
        for block in range(0, rows, BLOCK):
            acc_buf[i % 2, block : block + BLOCK, start : start + TILE] = acc[block : block + BLOCK] * scales[i, block]

    def out_piece(i):
        for mate, out in enumerate((keep, send)):
            for q in range(4):
                for j in range(nq):
                    source = pl.multiple_of(j * heads + group(me, q, mate, turn) * OWN, OWN)
                    to = ((q * count + i) * nq + j) * OWN
                    for k in range(kvr // 128):
                        at = k * 4 * count * nq * OWN + to
                        out[at : at + OWN, :] = acc_buf[i % 2, pl.ds(source, OWN), k * 128 : (k + 1) * 128]
        for part in range(rows // 128):
            for out in (keep, send):
                at = out.shape[0] - OWN + i * (rows // 128) + part
                out[at : at + 1, :] = tails[i, part]

    def pieces(stage, i):
        if not 0 <= i < count:
            return []
        if stage == 0:
            return [functools.partial(score_piece, i, t) for t in range(0, tokens, TILE)]
        if stage == 1:
            return [functools.partial(weight_piece, i, t) for t in range(0, rows, BLOCK)]
        return [functools.partial(value_piece, i, t) for t in range(0, kvr, TILE)] + [functools.partial(out_piece, i)]

    for i in range(count + 2):
        stages = [pieces(stage, i - stage) for stage in range(3)]
        marked = []
        for stage, own in enumerate(stages):
            marked += [((k + 0.5) / len(own), stage, k, piece) for k, piece in enumerate(own)]
        for _, _, _, piece in sorted(marked, key=lambda entry: entry[:3]):
            piece()
    for copy in ahead:
        copy.wait()


def attention(me, lengths, queries, cache, kvr, first, count, turn, ready, following, after, length):
    batch, nq, heads, lat = queries.shape
    tokens = cache.shape[2]
    rows = nq * heads
    out_rows = kvr // 128 * count * rows // 2 + OWN
    scratch = [
        pltpu.VMEM((2, rows, tokens), jnp.float32),
        pltpu.VMEM((2, rows, tokens), jnp.bfloat16),
        pltpu.VMEM((2, rows, kvr), jnp.float32),
        pltpu.SMEM((batch,), jnp.int32),
        pltpu.SemaphoreType.DMA,
        pltpu.SemaphoreType.DMA((max(following, 1), PIECES + 1)),
    ]
    if not ready:
        scratch += [
            pltpu.VMEM((count, nq, heads, lat), jnp.bfloat16),
            pltpu.VMEM((count, lat, tokens), jnp.bfloat16),
            pltpu.SemaphoreType.DMA((count, PIECES + 1)),
        ]
    out_shape = [jax.ShapeDtypeStruct((out_rows, 128), jnp.float32)] * 2
    if following:
        out_shape += [
            jax.ShapeDtypeStruct((following, nq, heads, lat), jnp.bfloat16),
            jax.ShapeDtypeStruct((following, lat, tokens), jnp.bfloat16),
        ]
    return pl.pallas_call(
        functools.partial(attention_kernel, first, count, turn, len(ready) > 0, following, len(after)),
        in_specs=[SM, HB, HB, HB] + [VM] * len(ready) + [ANY] * len(after),
        out_specs=[VM] * len(out_shape),
        out_shape=out_shape,
        scratch_shapes=scratch,
        compiler_params=pltpu.CompilerParams(vmem_limit_bytes=24 * MIB),
        cost_estimate=declared(length),
    )(me, lengths, queries, cache, *ready, *after)


def merged(refs, shares):
    logs = [ref[ref.shape[0] - OWN :, :] for ref in refs]
    largest = functools.reduce(jnp.maximum, logs)
    parts = [jnp.exp(log - largest) for log in logs]
    total = sum(parts[1:], parts[0])
    for k, part in enumerate(parts):
        shares[k] = (part / total).T
    return largest + jnp.log(total)


def merged_rows(refs, shares, me, sizes, places, q, b, j, turn):
    batch, nq, heads = sizes
    line, within = divmod(b * nq * heads + j * heads, 128)
    at = pl.ds(pl.multiple_of(within + group(me, q, 0, turn) * OWN, OWN), OWN)
    columns = [shares[k, at, line : line + 1] for k in range(len(refs))]
    height = places * batch * nq * OWN
    source = ((q * batch + b) * nq + j) * OWN
    for start in range(source, refs[0].shape[0] - OWN, height):
        terms_of = [column * ref[start : start + OWN, :] for column, ref in zip(columns, refs)]
        yield sum(terms_of[1:], terms_of[0])


def combine_kernel(places, pieces, sizes, turn, me_ref, keep_ref, got_ref, *refs):
    *outs, shares = refs[len(refs) - pieces - 1 :]
    lse = merged((keep_ref, got_ref), shares)
    batch, nq, _ = sizes
    size = batch * nq * OWN
    for q in range(places):
        side, at = divmod(q, places // pieces)
        for b in range(batch):
            for j in range(nq):
                blocks = merged_rows((keep_ref, got_ref), shares, me_ref[0], sizes, places, q, b, j, turn)
                for k, block in enumerate(blocks):
                    to = (k * (places // pieces) + at) * size + (b * nq + j) * OWN
                    outs[side][to : to + OWN, :] = block
    for out in outs:
        out[out.shape[0] - OWN :, :] = lse


def combine(me, keep, got, places, pieces, sizes, turn, after, length):
    out_rows = (keep.shape[0] - OWN) // pieces + OWN
    return pl.pallas_call(
        functools.partial(combine_kernel, places, pieces, sizes, turn),
        in_specs=[SM, VM, VM] + [ANY] * len(after),
        out_specs=[VM] * pieces,
        out_shape=[jax.ShapeDtypeStruct((out_rows, 128), jnp.float32)] * pieces,
        scratch_shapes=[pltpu.VMEM((2, 128, OWN), jnp.float32)],
        compiler_params=pltpu.CompilerParams(vmem_limit_bytes=16 * MIB),
        cost_estimate=declared(length),
    )(me, keep, got, *after)


def order_kernel(*refs):
    refs[-1][...] = jnp.zeros(refs[-1].shape, jnp.float32)


def order(after, length):
    return pl.pallas_call(
        order_kernel,
        in_specs=[ANY] * len(after),
        out_specs=VM,
        out_shape=jax.ShapeDtypeStruct((OWN, 128), jnp.float32),
        compiler_params=pltpu.CompilerParams(vmem_limit_bytes=MIB),
        cost_estimate=declared(length),
    )(*after)


def attend_rows(sizes, me, refs, shares, attended):
    merged(refs, shares)
    batch, nq, _ = sizes
    for b in range(batch):
        for j in range(nq):
            to = (b * nq + j) * OWN
            for k, block in enumerate(merged_rows(refs, shares, me, sizes, 1, 0, b, j, 0)):
                attended[k, to : to + OWN, :] = block


def attended_shape(array, sizes):
    rows = sizes[0] * sizes[1] * OWN
    return ((array.shape[0] - OWN) // rows, rows, 128)


def last_merge_kernel(sizes, count, me_ref, *refs):
    out_ref, shares = refs[-2:]
    attend_rows(sizes, me_ref[0], refs[:count], shares, out_ref)


def last_merge(me, arrays, sizes, after, length):
    return pl.pallas_call(
        functools.partial(last_merge_kernel, sizes, len(arrays)),
        in_specs=[SM] + [VM] * len(arrays) + [ANY] * len(after),
        out_specs=VM,
        out_shape=jax.ShapeDtypeStruct(attended_shape(arrays[0], sizes), jnp.float32),
        scratch_shapes=[pltpu.VMEM((len(arrays), 128, OWN), jnp.float32)],
        compiler_params=pltpu.CompilerParams(vmem_limit_bytes=16 * MIB),
        cost_estimate=declared(length),
    )(me, *arrays, *after)


def heads_kernel(sizes, count, me_ref, *refs):
    early, refs = refs[: -count - 4], refs[-count - 4 :]
    arrays, (up_ref, out_ref, shares, attended) = refs[:count], refs[count:]
    attend_rows(sizes, me_ref[0], arrays, shares, attended)
    width = up_ref.shape[2]
    for i in range(OWN):
        own = [
            jnp.concatenate([ref[k, pl.ds(i, ref.shape[1] // OWN, stride=OWN), :] for k in range(ref.shape[0])], axis=1)
            for ref in (*early, attended)
        ]
        own = jnp.concatenate(own, axis=0).astype(jnp.bfloat16)
        head_out = jnp.dot(own, up_ref[i], preferred_element_type=jnp.float32)
        out_ref[:, i * width : (i + 1) * width] = head_out.astype(jnp.bfloat16)


def heads_out(me, early, arrays, sizes, value_up):
    shape = attended_shape(arrays[0], sizes)
    places = sum(array.shape[1] for array in early) // OWN + shape[1] // OWN
    return pl.pallas_call(
        functools.partial(heads_kernel, sizes, len(arrays)),
        in_specs=[SM] + [VM] * (len(early) + len(arrays) + 1),
        out_specs=VM,
        out_shape=jax.ShapeDtypeStruct((places, OWN * value_up.shape[2]), jnp.bfloat16),
        scratch_shapes=[pltpu.VMEM((len(arrays), 128, OWN), jnp.float32), pltpu.VMEM(shape, jnp.float32)],
        compiler_params=pltpu.CompilerParams(vmem_limit_bytes=16 * MIB),
        cost_estimate=declared(0),
    )(me, *early, *arrays, value_up)


def terms_kernel(mate, places, me_ref, heads_ref, weights_ref, *refs):
    out_ref = refs[-1]
    heads = heads_ref[...]
    width = out_ref.shape[2]
    for at, q in enumerate(places):
        start = pl.multiple_of(group(me_ref[0], q, mate, 0) * width, width)
        out_ref[at] = jnp.dot(heads, weights_ref[:, pl.ds(start, width)], preferred_element_type=jnp.float32)


def terms(me, heads, weights, mate, places, width, after, length):
    return pl.pallas_call(
        functools.partial(terms_kernel, mate, places),
        in_specs=[SM, VM, VM] + [ANY] * len(after),
        out_specs=VM,
        out_shape=jax.ShapeDtypeStruct((len(places), heads.shape[0], width), jnp.float32),
        compiler_params=pltpu.CompilerParams(vmem_limit_bytes=20 * MIB),
        cost_estimate=declared(length),
    )(me, heads, weights, *after)


def fold_kernel(own_ref, got_ref, *refs):
    for q, out in enumerate(refs[len(refs) - own_ref.shape[0] :]):
        out[...] = own_ref[q] + got_ref[q]


def fold(own, got, after):
    return pl.pallas_call(
        fold_kernel,
        in_specs=[VM, VM] + [ANY] * len(after),
        out_specs=[VM] * own.shape[0],
        out_shape=[jax.ShapeDtypeStruct(own.shape[1:], jnp.float32)] * own.shape[0],
        compiler_params=pltpu.CompilerParams(vmem_limit_bytes=8 * MIB),
        cost_estimate=declared(0),
    )(own, got, *after)


def finish_kernel(*refs):
    ins, out_ref = refs[:-1], refs[-1]
    batch, nq, _ = out_ref.shape
    total = ins[0][...]
    for ref in ins[1:]:
        total = total + ref[...]
    total = total.astype(jnp.bfloat16)
    for b in range(batch):
        out_ref[b] = total[b * nq : (b + 1) * nq, :]


def finish(terms_of, batch, nq):
    return pl.pallas_call(
        finish_kernel,
        in_specs=[VM] * len(terms_of),
        out_specs=VM,
        out_shape=jax.ShapeDtypeStruct((batch, nq, terms_of[0].shape[1]), jnp.bfloat16),
        compiler_params=pltpu.CompilerParams(vmem_limit_bytes=8 * MIB),
        cost_estimate=declared(0),
    )(*terms_of)


def local(n, queries, latent_cache, context_lengths, value_up, output_projection_rows):
    batch, nq, heads, _ = queries.shape
    kvr = value_up.shape[1]
    me = lax.axis_index("seq").astype(jnp.int32).reshape(1)
    queries = pltpu.with_memory_space_constraint(queries, pltpu.HBM)
    cache = pltpu.with_memory_space_constraint(jnp.swapaxes(latent_cache, 1, 2), pltpu.HBM)
    lengths = pltpu.with_memory_space_constraint(context_lengths, pltpu.HBM)

    def swap(array, step, turn=0):
        return lax.ppermute(array, "seq", pairs_of(n, step, turn))

    keep, send, early = {}, {}, {}

    def arrived(p):
        turn = p & 1
        if len(send[p]) == 1:
            return [keep[p], swap(send[p][0], 2, turn)]
        second, first, both = send[p]
        return [keep[p], swap(first, 1, turn), swap(second, 2, turn), swap(both, 3, turn)]

    after, ready = (), ()
    for entry in ORDER.split():
        kind, p, length = entry[0], int(entry[1]), int(entry[3:])
        turn, sizes = p & 1, (PARTS[p], nq, heads)
        if kind == "N":
            after = (order(after, length),)
        elif kind == "A":
            following = (*PARTS, 0)[p + 1]
            outs = attention(
                me, lengths, queries, cache, kvr, sum(PARTS[:p]), PARTS[p], turn, ready, following, after, length
            )
            keep[p], send[p], ready = outs[0], outs[1:2], outs[2:]
            after = (keep[p],)
        elif kind == "M":
            early[p] = last_merge(me, arrived(p), sizes, after, length)
            after = (early[p],)
        else:
            step = "CS".index(kind)
            pieces = 4 if kind == "C" and p in DIRECT else 2
            keep[p], *send[p] = combine(
                me,
                keep[p],
                swap(send[p][0], step, turn),
                4 >> step,
                pieces,
                sizes,
                turn,
                after,
                length,
            )
            after = (keep[p],)

    last = len(PARTS) - 1
    flat = heads_out(me, [early[p] for p in range(last)], arrived(last), (PARTS[last], nq, heads), value_up)
    width = output_projection_rows.shape[1] // n
    sums = {}
    after = ()
    for places in ((3, 2), (1, 0)):
        sent = terms(me, flat, output_projection_rows, 1, places, width, after, LAST[0])
        own = terms(me, flat, output_projection_rows, 0, places, width, (sent,), LAST[1])
        after = (order((own,), LAST[2]),) if LAST[2] and after else ()
        folded = fold(own, swap(sent, 0), after)
        sums.update(zip(places, folded))
        after = (folded[0],)
    return finish([sums[0], swap(sums[3], 3), swap(sums[2], 1), swap(sums[1], 2)], batch, nq)


def plain(queries, latent_cache, context_lengths, value_up, output_projection_rows):
    batch, nq = queries.shape[:2]
    kvr = value_up.shape[1]
    tokens = latent_cache.shape[1]
    scores = score_scale * jnp.einsum("bqhc,btc->bqht", queries, latent_cache, preferred_element_type=jnp.float32)
    position = lax.axis_index("seq") * tokens + jnp.arange(tokens, dtype=jnp.int32)
    limit = context_lengths[:, None] - (nq - 1) + jnp.arange(nq, dtype=jnp.int32)[None, :]
    visible = position[None, None, None, :] < limit[:, :, None, None]
    masked = jnp.where(visible, scores, empty_mark)
    peak = jnp.max(masked, axis=3)
    weights = jnp.where(visible, jnp.exp(masked - peak[..., None]), 0.0)
    total = jnp.maximum(jnp.sum(weights, axis=3), 1.0)
    values = jnp.einsum(
        "bqht,btc->bqhc", weights.astype(jnp.bfloat16), latent_cache[:, :, :kvr], preferred_element_type=jnp.float32
    )
    partials = lax.all_to_all((values / total[..., None])[None], "seq", split_axis=3, concat_axis=0, tiled=True)
    lse = lax.all_to_all((peak + jnp.log(total))[None], "seq", split_axis=3, concat_axis=0, tiled=True)
    shares = jnp.exp(lse - jnp.max(lse, axis=0)[None])
    attended = jnp.sum(shares[..., None] * partials, axis=0) / jnp.sum(shares, axis=0)[..., None]
    head_out = jnp.einsum(
        "bqhc,hcv->bqhv", attended.astype(jnp.bfloat16), value_up, preferred_element_type=jnp.float32
    )
    flat = head_out.astype(jnp.bfloat16).reshape(batch, nq, -1)
    term = jnp.einsum("msp,pc->msc", flat, output_projection_rows, preferred_element_type=jnp.float32)
    return lax.psum_scatter(term, "seq", scatter_dimension=2, tiled=True).astype(jnp.bfloat16)


def solution(mesh):
    n = mesh.shape["seq"]

    def body(queries, latent_cache, context_lengths, value_up, output_projection_rows):
        args = (queries, latent_cache, context_lengths, value_up, output_projection_rows)
        if n == 8 and value_up.shape[0] == OWN:
            return local(n, *args)
        return plain(*args)

    placed = (
        P("grp", None, None, None),
        P("grp", "seq", None),
        P("grp"),
        P("seq", None, None),
        P("seq", None),
    )
    return jax.shard_map(
        body, mesh=mesh, in_specs=placed, out_specs=P("grp", None, "seq"), check_vma=False
    )
```
